256 devices in a mesh: segment: 8 (over z), expert: 8 (over y, core), dp: 4 (over x).
Axes of the slice: x: 4, y: 4, z: 8, core: 2. Of those that a mesh axis runs over, the one named last changes fastest.
Arguments:
- state_in: bfloat16 [8, 4, 4096, 2048], P('segment', None, ('expert', 'dp')), may hold values from -6 to 6
- entering: bfloat16 [1, 4, 4096, 2048], P(None, None, ('expert', 'dp')), may hold values from -6 to 6
- saved: bfloat16 [8, 2, 2, 4096, 2048], P('segment', None, None, ('expert', 'dp')), may hold values from -6 to 6
- route_ids: int32 [8, 2, 4, 2, 4096, 6], P('segment', None, None, None, ('expert', 'dp')), may hold values from 0 to 63, as said below
- gate_vals: float32 [8, 2, 4, 2, 4096, 6], P('segment', None, None, None, ('expert', 'dp')), may hold values from 0.25 to 1
- w_gate: bfloat16 [8, 8, 2048, 1408], P('segment', 'expert', None, 'dp'), may hold values from -0.125 to 0.125
- w_up: bfloat16 [8, 8, 2048, 1408], P('segment', 'expert', None, 'dp'), may hold values from -0.125 to 0.125
- w_down: bfloat16 [8, 8, 1408, 2048], P('segment', 'expert', 'dp'), may hold values from -0.15625 to 0.15625
- gains: float32 [8, 2, 2048], P('segment'), may hold values from 0.5 to 2
Outputs:
- state_out: bfloat16 [8, 4, 4096, 2048], P('segment', None, ('expert', 'dp'))
The draws below stay inside these ranges and needn't reach their ends.
Inputs may be any that keep to these rules, and one draw needn't show every extreme that they name: `route_ids`: the ids of one token are distinct, and a token names at most one id under 4. Within each block of 128 consecutive tokens (the tokens of one device) an id under 4 is named by at most 8 tokens. For every section, slot, unit and sublayer some id under 4 is named by exactly 8 tokens in every block, and every block has an id under 4 named by exactly 8 of its tokens.
All inputs are finite; a program needn't handle non-finite values.
Results may differ from the reference program's by a relative error of at most 0.017.
Values may be sent and summed in bfloat16 or wider, within the bound.
No kernel may reach another device: no remote copies, remote signals or barrier semaphores. Data moves between devices by JAX's collectives and lax.ppermute only.
A program may use at most 128 MiB of HBM per device.

```python
import math
import jax
import jax.numpy as jnp
from jax import lax

D = 2048
FF = 1408
ROUTED = 64
TOPK = 6
TOK = 128
CAP = 8
SLOTS = 2
EXPERTS = 4
FFQ = 352
TOKENS = 4096
SEGMENTS = 8
N_DP = 4


def draw_route_ids(key, part):
    leading = SEGMENTS * SLOTS * 4 * 2
    blocks = TOKENS // TOK
    subkeys = jax.random.split(jax.random.fold_in(key, 11), 6)
    counts = jax.random.randint(subkeys[0], (leading, blocks, EXPERTS), 0, CAP + 1)
    busiest = jax.random.randint(subkeys[1], (leading, 1, 1), 0, EXPERTS)
    second = jax.random.randint(subkeys[2], (leading, blocks, 1), 0, EXPERTS)
    experts = jnp.arange(EXPERTS, dtype=jnp.int32)
    counts = jnp.where((experts[None, None, :] == busiest) | (experts[None, None, :] == second), CAP, counts)
    starts = jnp.cumsum(counts, axis=-1) - counts
    order_keys = jax.random.split(subkeys[3], leading * blocks)
    places = jax.vmap(lambda subkey: jax.random.permutation(subkey, TOK))(order_keys).reshape(leading, blocks, TOK)
    inside = (places[:, :, :, None] >= starts[:, :, None, :]) & (places[:, :, :, None] < (starts + counts)[:, :, None, :])
    has_route = jnp.sum(inside.astype(jnp.int32), axis=-1)
    chosen = jnp.sum(jnp.where(inside, experts, 0), axis=-1)
    others = ROUTED - EXPERTS
    scores = jax.random.randint(subkeys[4], (leading, blocks, TOK, others), 0, 1 << 20) * others + jnp.arange(others, dtype=jnp.int32)
    ignored, picked = lax.top_k(scores, TOPK)
    filler = picked.astype(jnp.int32) + EXPERTS
    column = jax.random.randint(subkeys[5], (leading, blocks, TOK, 1), 0, TOPK)
    positions = jnp.arange(TOPK, dtype=jnp.int32)
    route_ids = jnp.where((has_route[..., None] == 1) & (positions == column), chosen[..., None], filler)
    return route_ids.reshape(SEGMENTS, SLOTS, 4, 2, TOKENS, TOPK)


def shard_levels(key, dims, cuts, smallest, top_value):
    def one(position, parts):
        heights = jax.random.uniform(jax.random.fold_in(jax.random.fold_in(key, 6), position), (parts,), jnp.float32, smallest / len(cuts), top_value / len(cuts))
        return jnp.repeat(jnp.exp(heights), dims[position] // parts).reshape((-1,) + (1,) * (len(dims) - position - 1))

    loudness = one(*cuts[0])
    for cut in cuts[1:]:
        loudness = loudness * one(*cut)
    return loudness


def noise(key, extent, width, limit, cuts=(), held_as=jnp.bfloat16):
    level = shard_levels(key, extent, cuts, -0.22, 0.18) if cuts else 1.0
    values = jax.random.normal(key, extent, jnp.float32) * width * level
    return jnp.minimum(jnp.maximum(values, -limit), limit).astype(held_as)


def setup_inputs(seed: int = 0) -> dict:
    arg_keys = jax.random.split(jax.random.key(seed), 10)
    return {
        "state_in": noise(arg_keys[0], (SEGMENTS, 4, TOKENS, D), 1.0, 6.0, ((0, 8), (2, 32))),
        "entering": noise(arg_keys[1], (SLOTS - 1, 4, TOKENS, D), 1.0, 6.0, ((2, 32),)),
        "saved": noise(arg_keys[2], (SEGMENTS, SLOTS, 2, TOKENS, D), 1.0, 6.0, ((0, 8), (3, 32))),
        "route_ids": draw_route_ids(jax.random.fold_in(arg_keys[9], 71), 0),
        "gate_vals": jnp.clip(0.25 + 0.75 * jax.random.uniform(arg_keys[4], (SEGMENTS, SLOTS, 4, 2, TOKENS, TOPK), jnp.float32) ** shard_levels(arg_keys[4], (SEGMENTS, SLOTS, 4, 2, TOKENS, TOPK), ((0, 8), (4, 32)), -0.2, 0.2), 0.25, 1.0),
        "w_gate": noise(arg_keys[5], (SEGMENTS, 2 * EXPERTS, D, FF), D ** -0.5, 0.125, ((0, 8), (1, 8), (3, 4))),
        "w_up": noise(arg_keys[6], (SEGMENTS, 2 * EXPERTS, D, FF), D ** -0.5, 0.125, ((0, 8), (1, 8), (3, 4))),
        "w_down": noise(arg_keys[7], (SEGMENTS, 2 * EXPERTS, FF, D), FF ** -0.5, 0.15625, ((0, 8), (1, 8), (2, 4))),
        "gains": jnp.clip(jnp.exp(math.log(2.0) - 1.3862944 * jax.random.uniform(arg_keys[8], (SEGMENTS, 2, D), jnp.float32) ** shard_levels(arg_keys[8], (SEGMENTS, 2, D), ((0, 8),), -0.2, 0.2)), 0.5, 2.0),
    }


EPSILON = 1e-06
HIGHEST = lax.Precision.HIGHEST
CONTRACT_LAST = (((1,), (1,)), ((), ()))

def route_tables(block_ids, block_gates):
    expert_range = jnp.arange(EXPERTS, dtype=jnp.int32)
    matches = block_ids[:, :, None] == expert_range[None, None, :]
    routed = lax.optimization_barrier(jnp.sum(matches.astype(jnp.int32), axis=1))
    weighting = lax.optimization_barrier(jnp.sum(jnp.where(matches, block_gates[:, :, None], jnp.zeros_like(block_gates[:, :, None])), axis=1))
    earlier = jnp.cumsum(routed, axis=0) - routed
    slot_range = jnp.arange(CAP, dtype=jnp.int32)
    chosen = (routed[:, :, None] == 1) & (earlier[:, :, None] == slot_range[None, None, :])
    row_total = block_ids.shape[0]
    selector = jnp.transpose(chosen.reshape(row_total, EXPERTS * CAP)).astype(block_gates.dtype)
    slot_gate = lax.optimization_barrier(jnp.sum(jnp.where(chosen, weighting[:, :, None], jnp.zeros_like(weighting[:, :, None])), axis=0))
    return (selector, slot_gate.reshape(EXPERTS * CAP))

def tables_of(unit_ids, unit_gates):
    blocks = TOKENS // TOK
    return jax.vmap(route_tables)(unit_ids.reshape(blocks, TOK, TOPK), unit_gates.reshape(blocks, TOK, TOPK))

def norm_rows(values, norm_gain):
    inverse_rms = lax.rsqrt(lax.optimization_barrier(jnp.mean(values * values, axis=-1, keepdims=True)) + EPSILON)
    return ((values * inverse_rms * norm_gain).astype(jnp.bfloat16), inverse_rms)

def norm_back(values, inverse_rms, norm_gain, delta, grad_normed):
    weighted = norm_gain * grad_normed
    cubed = inverse_rms * inverse_rms * inverse_rms
    return delta + inverse_rms * weighted - values * cubed * lax.optimization_barrier(jnp.sum(weighted * values, axis=-1, keepdims=True)) / values.shape[-1]

def select_rows(selector, values):
    blocks = TOKENS // TOK
    return jnp.einsum('bst,btd->bsd', selector, values.reshape(blocks, TOK, D).astype(selector.dtype), precision=HIGHEST)

def spread_rows(selector, slot_values):
    return jnp.einsum('bst,bsd->btd', selector, slot_values, precision=HIGHEST).reshape(TOKENS, D)

def expert_slice(slot_rows, expert_index):
    blocks = TOKENS // TOK
    return slot_rows.reshape(blocks, EXPERTS, CAP, D)[:, expert_index].reshape(blocks * CAP, D)

def expert_forward(hidden_rows, gate_weight, up_weight):
    gate_pre = jnp.dot(hidden_rows, gate_weight, preferred_element_type=jnp.float32)
    up_pre = jnp.dot(hidden_rows, up_weight, preferred_element_type=jnp.float32)
    return (gate_pre, up_pre)

def expert_back(grad_in_rows, gate_pre, up_pre, gate_weight, up_weight, down_weight):
    grad_act = lax.dot_general(grad_in_rows, down_weight, CONTRACT_LAST, preferred_element_type=jnp.float32)
    sigmoid_gate = jax.nn.sigmoid(gate_pre)
    grad_gate = (grad_act * up_pre * sigmoid_gate * (1.0 + gate_pre * (1.0 - sigmoid_gate))).astype(jnp.bfloat16)
    grad_up = (grad_act * gate_pre * sigmoid_gate).astype(jnp.bfloat16)
    grad_hidden = lax.dot_general(grad_gate, gate_weight, CONTRACT_LAST, preferred_element_type=jnp.float32)
    grad_hidden = grad_hidden + lax.dot_general(grad_up, up_weight, CONTRACT_LAST, preferred_element_type=jnp.float32)
    return grad_hidden.astype(jnp.bfloat16)

def sublayer(values, unit_ids, unit_gates, layer):
    gate_all, up_all, down_all, norm_gain = layer
    blocks = TOKENS // TOK
    selector, slot_gate = tables_of(unit_ids, unit_gates)
    normed, inverse_rms = norm_rows(values, norm_gain)
    slot_rows = select_rows(selector, normed).astype(jnp.bfloat16)
    outputs = []
    for expert_index in range(EXPERTS):
        hidden_rows = expert_slice(slot_rows, expert_index)
        gate_pre, up_pre = expert_forward(hidden_rows, gate_all[expert_index], up_all[expert_index])
        activation = (jax.nn.silu(gate_pre) * up_pre).astype(jnp.bfloat16)
        summed = jnp.zeros((hidden_rows.shape[0], D), jnp.float32)
        for quarter in range(N_DP):
            offset = quarter * FFQ
            partial_value = jnp.dot(activation[:, offset:offset + FFQ], down_all[expert_index, offset:offset + FFQ], preferred_element_type=jnp.float32).astype(jnp.bfloat16)
            summed = summed + lax.optimization_barrier(partial_value).astype(jnp.float32)
        outputs.append(summed.reshape(blocks, CAP, D))
    expert_out = jnp.stack(outputs, axis=1).reshape(blocks, EXPERTS * CAP, D)
    return values + spread_rows(selector, slot_gate[:, :, None] * expert_out)

def sublayer_back(values, delta, unit_ids, unit_gates, layer):
    gate_all, up_all, down_all, norm_gain = layer
    blocks = TOKENS // TOK
    selector, slot_gate = tables_of(unit_ids, unit_gates)
    normed, inverse_rms = norm_rows(values, norm_gain)
    slot_rows = select_rows(selector, normed).astype(jnp.bfloat16)
    slot_grads = (slot_gate[:, :, None] * select_rows(selector, delta)).astype(jnp.bfloat16)
    outputs = []
    for expert_index in range(EXPERTS):
        hidden_rows = expert_slice(slot_rows, expert_index)
        grad_in_rows = expert_slice(slot_grads, expert_index)
        gate_pre, up_pre = expert_forward(hidden_rows, gate_all[expert_index], up_all[expert_index])
        summed = jnp.zeros((hidden_rows.shape[0], D), jnp.float32)
        for quarter in range(N_DP):
            offset = quarter * FFQ
            partial_value = expert_back(grad_in_rows, gate_pre[:, offset:offset + FFQ], up_pre[:, offset:offset + FFQ], gate_all[expert_index][:, offset:offset + FFQ], up_all[expert_index][:, offset:offset + FFQ], down_all[expert_index, offset:offset + FFQ])
            summed = summed + lax.optimization_barrier(partial_value).astype(jnp.float32)
        outputs.append(summed.reshape(blocks, CAP, D))
    grad_normed = spread_rows(selector, jnp.stack(outputs, axis=1).reshape(blocks, EXPERTS * CAP, D))
    return norm_back(values, inverse_rms, norm_gain, delta, grad_normed)

def forward_unit(start, unit_ids, unit_gates, layers, order):
    values = start.astype(jnp.float32)
    for sub_index in order:
        values = sublayer(values, unit_ids[sub_index], unit_gates[sub_index], layers[sub_index])
    return values.astype(jnp.bfloat16)

def backward_unit(kept, incoming, unit_ids, unit_gates, layers, order):
    first_sub = order[0]
    second_sub = order[1]
    start = kept.astype(jnp.float32)
    middle = sublayer(start, unit_ids[first_sub], unit_gates[first_sub], layers[first_sub])
    grad_middle = sublayer_back(middle, incoming.astype(jnp.float32), unit_ids[second_sub], unit_gates[second_sub], layers[second_sub])
    grad_start = sublayer_back(start, grad_middle, unit_ids[first_sub], unit_gates[first_sub], layers[first_sub])
    return grad_start.astype(jnp.bfloat16)

def reference(state_in, entering, saved, route_ids, gate_vals, w_gate, w_up, w_down, gains):
    current = state_in
    result = state_in
    for slot_index in range(SLOTS):
        produced = []
        for segment_index in range(SEGMENTS):
            layers = [(w_gate[segment_index, sub_index * EXPERTS:(sub_index + 1) * EXPERTS], w_up[segment_index, sub_index * EXPERTS:(sub_index + 1) * EXPERTS], w_down[segment_index, sub_index * EXPERTS:(sub_index + 1) * EXPERTS], gains[segment_index, sub_index]) for sub_index in range(2)]
            ids_here = route_ids[segment_index, slot_index]
            gates_here = gate_vals[segment_index, slot_index]
            first_forward = forward_unit(current[segment_index, 0], ids_here[0], gates_here[0], layers, (0, 1))
            second_forward = forward_unit(current[segment_index, 1], ids_here[1], gates_here[1], layers, (1, 0))
            first_backward = backward_unit(saved[segment_index, slot_index, 0], current[segment_index, 2], ids_here[2], gates_here[2], layers, (0, 1))
            second_backward = backward_unit(saved[segment_index, slot_index, 1], current[segment_index, 3], ids_here[3], gates_here[3], layers, (1, 0))
            produced.append(jnp.stack([first_forward, second_forward, first_backward, second_backward]))
        result = jnp.stack(produced)
        if slot_index + 1 < SLOTS:
            arriving = entering[slot_index]
            acts_up = jnp.concatenate([arriving[0][None], result[:-1, 0]], axis=0)
            acts_down = jnp.concatenate([result[1:, 1], arriving[1][None]], axis=0)
            grads_down = jnp.concatenate([result[1:, 2], arriving[2][None]], axis=0)
            grads_up = jnp.concatenate([arriving[3][None], result[:-1, 3]], axis=0)
            current = jnp.stack([acts_up, acts_down, grads_down, grads_up], axis=1)
    return result
```

```python
import functools

import jax
import jax.numpy as jnp
from jax import lax
from jax.experimental import pallas as pl
from jax.experimental.pallas import tpu as pltpu
from jax.sharding import PartitionSpec as P

CAP = 8
EPSILON = 1e-06
CHUNK = 256
F32 = jnp.float32
BF16 = jnp.bfloat16
NT = (((1,), (1,)), ((), ()))
VMEM_LIMIT = 48 * 1024 * 1024


def dot(a, b):
    return jnp.dot(a, b, preferred_element_type=F32)


def dot_nt(a, b):
    return lax.dot_general(a, b, NT, preferred_element_type=F32)


def whole(shape):
    zeros = (0,) * len(shape)
    return pl.BlockSpec(tuple(shape), lambda i: zeros, memory_space=pltpu.VMEM)


def item(shape, index):
    place = tuple(index) + (0,) * (len(shape) - len(index))
    block = (None,) * len(index) + tuple(shape[len(index):])
    return pl.BlockSpec(block, lambda i: place, memory_space=pltpu.VMEM)


def call(body, operands, out_shapes, scratch, flops, limit=VMEM_LIMIT):
    arrays = [a for a, _ in operands]
    moved = sum(o.size * o.dtype.itemsize for o in out_shapes)
    moved += sum(min(a.size * a.dtype.itemsize, 2**20) for a in arrays)
    return pl.pallas_call(
        body,
        grid=(1,),
        out_shape=out_shapes,
        in_specs=[s for _, s in operands],
        out_specs=[whole(o.shape) for o in out_shapes],
        scratch_shapes=scratch,
        compiler_params=pltpu.CompilerParams(vmem_limit_bytes=limit),
        cost_estimate=pl.CostEstimate(flops=flops, bytes_accessed=moved, transcendentals=0),
    )(*arrays)


def tables_body(place_ref, ids_ref, gates_ref, pick_ref, spread_ref, gate_ref):
    count = ids_ref.shape[0]
    tokens = ids_ref.shape[2]
    half = tokens // 2
    rows = 8 * CAP
    at_bottom = place_ref[0]
    at_top = place_ref[1]
    row = lax.broadcasted_iota(jnp.int32, (rows, tokens), 0)
    lane = lax.broadcasted_iota(jnp.int32, (rows, tokens), 1)
    dest = row >> 3
    slot = (row & 7).astype(F32)
    expert = dest & 3
    dest_sub = dest >> 2
    stream = (lane >= half).astype(jnp.int32)
    t0 = lax.broadcasted_iota(jnp.int32, (tokens, tokens), 0)
    t1 = lax.broadcasted_iota(jnp.int32, (tokens, tokens), 1)
    before = ((t0 < t1) & ((t0 >= half) == (t1 >= half))).astype(F32).astype(BF16)
    end_rows = jnp.where(dest < 4, at_bottom, at_top).astype(F32)

    def step(index, carry):
        order = index & 1
        ids = ids_ref[index]
        gates = gates_ref[index]
        routed = jnp.zeros((rows, tokens), F32)
        weight = jnp.zeros((rows, tokens), F32)
        for k in range(ids.shape[0]):
            hit = ids[k : k + 1, :] == expert
            routed = routed + hit.astype(F32)
            weight = weight + jnp.where(hit, gates[k : k + 1, :], 0.0)
        earlier = dot(routed.astype(BF16), before)
        good = (routed == 1.0) & (earlier == slot) & (dest_sub == (stream ^ order))
        chosen = good.astype(F32)
        weighted = jnp.where(good, weight, 0.0)
        pick_ref[index] = chosen.astype(BF16)
        turned = jnp.transpose(jnp.concatenate([chosen, weighted], axis=0))
        spread_ref[index] = turned[:, :rows].astype(BF16)
        side = lax.broadcasted_iota(jnp.int32, turned.shape, 1)
        gate_ref[index] = jnp.sum(jnp.where(side >= rows, turned, 0.0), axis=1, keepdims=True)
        return carry

    lax.fori_loop(0, count, step, 0)
    for source, target in ((4, count), (7, count + 1)):
        pick_ref[target] = (pick_ref[source].astype(F32) * end_rows).astype(BF16)


def make_tables(place, ids, gates):
    count, _, tokens = ids.shape
    rows = 8 * CAP
    return call(
        tables_body,
        [
            (place, pl.BlockSpec(memory_space=pltpu.SMEM)),
            (ids, whole(ids.shape)),
            (gates, whole(gates.shape)),
        ],
        [
            jax.ShapeDtypeStruct((count + 2, rows, tokens), BF16),
            jax.ShapeDtypeStruct((count, tokens, rows), BF16),
            jax.ShapeDtypeStruct((count, tokens, 1), F32),
        ],
        [],
        10**8,
    )


def by_half(value, first, second):
    half = value.shape[0] // 2
    return jnp.concatenate([value[:half] * first, value[half:] * second], axis=0)


def columns(index):
    return pl.ds(pl.multiple_of(index * CHUNK, CHUNK), CHUNK)


def block_rows(ref, block, cols):
    rows = ref[:, :, cols].astype(F32)[:, block * CAP : (block + 1) * CAP]
    return rows.reshape(ref.shape[0] * CAP, CHUNK).astype(BF16)


def put_rows(out, blocks, cols, first=0):
    for k in range(out.shape[0]):
        start = (first + k) * CAP
        parts = [b[start : start + CAP] for b in blocks]
        rows = parts[0] if len(parts) == 1 else jnp.concatenate(parts, axis=0)
        out[k, :, cols] = rows.astype(BF16)


def fold(value):
    total = value[:, :128]
    for start in range(128, value.shape[1], 128):
        total = total + value[:, start : start + 128]
    return total


def row_total(partial):
    return jnp.sum(partial, axis=-1, keepdims=True)


def inverse_rms(square_partial, width):
    return lax.rsqrt(row_total(square_partial) / width + EPSILON)


def steps_of(width):
    return width // CHUNK


def start_norm(x_ref):
    width = x_ref.shape[1]

    def step(index, total):
        v = x_ref[:, columns(index)].astype(F32)
        return total + fold(v * v)

    total = lax.fori_loop(0, steps_of(width), step, jnp.zeros((x_ref.shape[0], 128), F32))
    return inverse_rms(total, width)


def add_routes(x_ref, ret_refs, block, spread_ref, gate_ref, mid_ref):
    width = x_ref.shape[1]
    spread = spread_ref[...]
    gate = gate_ref[...]

    def step(index, total):
        cols = columns(index)
        m = x_ref[:, cols].astype(F32) + gate * dot(spread, block_rows(ret_refs, block, cols))
        mid_ref[:, cols] = m
        return total + fold(m * m)

    total = lax.fori_loop(0, steps_of(width), step, jnp.zeros((x_ref.shape[0], 128), F32))
    return inverse_rms(total, width)


def back_sums(load, ret_refs, block, spread_ref, gains, work_ref):
    height, width = work_ref.shape
    spread = spread_ref[...]

    def step(index, totals):
        cols = columns(index)
        grad = dot(spread, block_rows(ret_refs, block, cols))
        w = by_half(grad, gains[0][:, cols], gains[1][:, cols])
        work_ref[:, cols] = w
        v = load(cols)
        return (totals[0] + fold(w * v), totals[1] + fold(v * v))

    zero = jnp.zeros((height, 128), F32)
    along, square = lax.fori_loop(0, steps_of(width), step, (zero, zero))
    inv = inverse_rms(square, width)
    return (row_total(along) * (inv * inv * inv) / width, inv)


def local(state_in, entering, saved, route_ids, gate_vals, w_gate, w_up, w_down, gains):
    width = state_in.shape[-1]
    tokens = state_in.shape[-2]
    pair = 2 * tokens
    hidden = w_down.shape[-2]
    dp_count = lax.axis_size("dp")
    segment_count = lax.axis_size("segment")
    expert_devices = lax.axis_size("expert")
    section = lax.axis_index("segment").astype(jnp.int32)
    at_bottom = (section == 0).astype(jnp.int32)
    at_top = (section == segment_count - 1).astype(jnp.int32)
    place = jnp.stack([at_bottom, at_top])
    block_shape = lambda n: [jax.ShapeDtypeStruct((expert_devices, n * CAP, width), BF16)]
    full = (pair, width)

    cut = hidden // 2
    turned_up = jnp.transpose(w_up[0, 0])
    own_a = jnp.concatenate([jnp.transpose(w_gate[0, 0]), turned_up[:cut]])
    own_b = jnp.concatenate([turned_up[cut:], w_down[0, 0]])
    ahead = [(i, (i + 1) % dp_count) for i in range(dp_count)]
    behind = [((i + 1) % dp_count, i) for i in range(dp_count)]
    left_a = lax.ppermute(own_a, "dp", ahead)
    right_b = lax.ppermute(own_b, "dp", behind)
    left_b = lax.ppermute(own_b, "dp", ahead)
    right_a = lax.ppermute(own_a, "dp", behind)
    far_a = lax.ppermute(left_a, "dp", ahead)
    far_b = lax.ppermute(right_b, "dp", behind)
    weights = [own_a, own_b, left_a, left_b, right_a, right_b, far_a, far_b]

    def exchange(blocks):
        return lax.all_to_all(blocks, "expert", split_axis=0, concat_axis=0, tiled=True)

    upward = [(i, i + 1) for i in range(segment_count - 1)]
    downward = [(i + 1, i) for i in range(segment_count - 1)]

    def paired(values):
        turned = jnp.transpose(values[0], (0, 1, 4, 2, 3))
        stream_a = turned[:, 0::2]
        stream_b = jnp.flip(turned[:, 1::2], axis=3)
        both = jnp.concatenate([stream_a, stream_b], axis=4)
        both = jnp.transpose(both, (0, 1, 3, 2, 4))
        return both.reshape((8,) + both.shape[3:])

    ids = paired(route_ids).astype(F32)
    gates = paired(gate_vals)
    choices = ids.shape[1]
    gain_rows = gains[0].reshape(2, width // 128, 128)
    pack_down = jnp.concatenate(
        [ids[4, :, :tokens], ids[7, :, tokens:], gates[4, :, :tokens], gates[7, :, tokens:], gain_rows[0]]
    )
    pack_up = jnp.concatenate(
        [ids[7, :, :tokens], ids[4, :, tokens:], gates[7, :, :tokens], gates[4, :, tokens:], gain_rows[1]]
    )
    above = lax.ppermute(pack_down, "segment", downward)
    below = lax.ppermute(pack_up, "segment", upward)
    part = lambda v, i: v[i * choices : (i + 1) * choices]
    more_ids = jnp.stack(
        [
            jnp.concatenate([part(above, 0), part(below, 1)], axis=1),
            jnp.concatenate([part(below, 0), part(above, 1)], axis=1),
        ]
    )
    more_gates = jnp.stack(
        [
            jnp.concatenate([part(above, 2), part(below, 3)], axis=1),
            jnp.concatenate([part(below, 2), part(above, 3)], axis=1),
        ]
    )
    gain_above = above[4 * choices :].reshape(1, width)
    gain_below = below[4 * choices :].reshape(1, width)
    all_ids = jnp.concatenate([ids, more_ids]).astype(jnp.int32)
    all_gates = jnp.concatenate([gates, more_gates])
    picks, spreads, gate_columns = make_tables(place, all_ids, all_gates)

    pick = lambda t: (picks, item(picks.shape, (t,)))
    spread = lambda t: (spreads, item(spreads.shape, (t,)))
    gate = lambda t: (gate_columns, item(gate_columns.shape, (t,)))
    gain_lines = gains[0].reshape(2, 1, width)
    gain = lambda j: (gain_lines, item(gain_lines.shape, (j,)))
    plain = lambda a: (a, whole(a.shape))
    each = lambda arrays: [plain(a) for a in arrays]
    states = state_in.reshape(2, pair, width)
    state = lambda p: (states, item(states.shape, (p,)))
    keeps = saved.reshape(2, pair, width)
    kept = lambda t: (keeps, item(keeps.shape, (t,)))
    enters = entering.reshape(2, pair, width)
    enter = lambda p: (enters, item(enters.shape, (p,)))
    place_in = (place, pl.BlockSpec(memory_space=pltpu.SMEM))
    big = pltpu.VMEM(full, F32)
    token_flops = 10**8

    def t1(*refs):
        xs, pick_refs = refs[0:4], refs[4:8]
        delta, pick_d, gate_d, ga, gb = refs[8:13]
        outs = refs[13]
        invs = [start_norm(x) for x in xs]

        def step(index, carry):
            cols = columns(index)
            blocks = []
            for x, inv, pick_x in zip(xs, invs, pick_refs):
                v = by_half(x[:, cols].astype(F32) * inv, ga[:, cols], gb[:, cols]).astype(BF16)
                blocks.append(dot(pick_x[...], v))
            g = (gate_d[...] * delta[:, cols].astype(F32)).astype(BF16)
            blocks.append(dot(pick_d[...], g))
            put_rows(outs, blocks, cols)
            return carry

        lax.fori_loop(0, steps_of(width), step, 0)

    (rows1,) = call(
        t1,
        [state(0), kept(0), kept(1), enter(0), pick(0), pick(2), pick(6), pick(10)]
        + [enter(1), pick(11), gate(7), gain(0), gain(1)],
        block_shape(5),
        [],
        2 * token_flops,
    )
    got1 = exchange(rows1)

    def owner(got, blocks, pre_blocks, forward_blocks, back_block, inner_block, kept_pre, keep_blocks, extra):
        out_blocks = forward_blocks + (back_block is not None)
        operands = [plain(got)]
        if extra is not None:
            operands += [plain(extra)]
        if kept_pre is not None:
            array_g, array_u, position = kept_pre
            spec = pl.BlockSpec(
                (dp_count, 64, hidden), lambda i: (0, position, 0), memory_space=pltpu.VMEM
            )
            operands += [(array_g, spec), (array_u, spec)]
        operands += [(w, pl.BlockSpec(memory_space=pl.ANY)) for w in weights]
        outs = block_shape(out_blocks)
        if keep_blocks:
            shape = jax.ShapeDtypeStruct((dp_count, 64 * len(keep_blocks), hidden), F32)
            outs += [shape, shape]

        def body(*refs):
            refs = list(refs)
            take = lambda n: [refs.pop(0) for _ in range(n)]
            ins = take(1)[0]
            extras = take(1)[0] if extra is not None else None
            pre_g, pre_u = take(2) if kept_pre is not None else (None, None)
            sources = take(2 * dp_count)
            out_refs = take(1)[0]
            keep_g, keep_u = take(2) if keep_blocks else (None, None)
            x, wg, wu, wd, acc, sems = refs

            def copies(q, a, b):
                part = lambda ref, start, size: ref.at[pl.ds(start, size)]
                pairs = [
                    (part(a, 0, hidden), wg.at[q]),
                    (part(a, hidden, cut), wu.at[q, pl.ds(0, cut)]),
                    (part(b, 0, cut), wu.at[q, pl.ds(cut, cut)]),
                    (part(b, cut, hidden), wd.at[q]),
                ]
                return [pltpu.make_async_copy(p, t, sems.at[i, q]) for i, (p, t) in enumerate(pairs)]

            for q in range(dp_count):
                for copy in copies(q, sources[2 * q], sources[2 * q + 1]):
                    copy.start()

            def load(index, carry):
                cols = columns(index)
                for b in range(blocks):
                    rows = block_rows(ins, b, cols)
                    if extras is not None:
                        rows = rows + block_rows(extras, 3 + b, cols)
                    x[b * 64 : (b + 1) * 64, cols] = rows
                acc[:, cols] = jnp.zeros((acc.shape[0], CHUNK), F32)
                return carry

            lax.fori_loop(0, steps_of(width), load, 0)

            def quarter(q, carry):
                for copy in copies(q, sources[0], sources[1]):
                    copy.wait()
                if pre_blocks:
                    rows = x[: pre_blocks * 64]
                    gate_pre = dot_nt(rows, wg[q])
                    up_pre = dot_nt(rows, wu[q])
                    for i, b in enumerate(keep_blocks):
                        keep_g[q, i * 64 : (i + 1) * 64] = gate_pre[b * 64 : (b + 1) * 64]
                        keep_u[q, i * 64 : (i + 1) * 64] = up_pre[b * 64 : (b + 1) * 64]
                if forward_blocks:
                    count = forward_blocks * 64
                    fg = gate_pre[:count]
                    act = (fg * jax.nn.sigmoid(fg) * up_pre[:count]).astype(BF16)
                    acc[:count] += dot(act, wd[q])
                if back_block is not None:
                    base = forward_blocks * 64
                    if kept_pre is not None:
                        bg, bu = pre_g[q], pre_u[q]
                    else:
                        bg = gate_pre[inner_block * 64 : (inner_block + 1) * 64]
                        bu = up_pre[inner_block * 64 : (inner_block + 1) * 64]
                    grad_act = dot_nt(x[back_block * 64 : (back_block + 1) * 64], wd[q])
                    sig = jax.nn.sigmoid(bg)
                    grad_gate = (grad_act * bu * sig * (1.0 + bg * (1.0 - sig))).astype(BF16)
                    grad_up = (grad_act * bg * sig).astype(BF16)
                    acc[base : base + 64] += dot(grad_gate, wg[q]) + dot(grad_up, wu[q])
                return carry

            lax.fori_loop(0, dp_count, quarter, 0)

            def store(index, carry):
                cols = columns(index)
                put_rows(out_refs, [acc[b * 64 : (b + 1) * 64, cols] for b in range(out_blocks)], cols)
                return carry

            lax.fori_loop(0, steps_of(width), store, 0)

        held_shape = pltpu.VMEM((dp_count, hidden, width), BF16)
        result = call(
            body,
            operands,
            outs,
            [
                pltpu.VMEM((blocks * 64, width), BF16),
                held_shape,
                held_shape,
                held_shape,
                pltpu.VMEM((out_blocks * 64, width), F32),
                pltpu.SemaphoreType.DMA((4, dp_count)),
            ],
            2 * 64 * width * hidden * dp_count * (2 * pre_blocks + forward_blocks + 3 * (back_block is not None)),
        )
        return result[0], tuple(result[1:])

    out1, kept_pre = owner(got1, 3, 3, 3, None, None, None, (1, 2), None)
    ret1 = exchange(out1)

    def t2(*refs):
        refs = list(refs)
        take = lambda n: [refs.pop(0) for _ in range(n)]
        rets = take(1)[0]
        xs = take(3)
        spread_refs = take(3)
        gate_refs = take(3)
        pick_refs = take(3)
        delta, gate_d, ga, gb = take(4)
        outs = take(1)[0]
        mids = take(3)
        invs = [
            add_routes(xs[i], rets, i, spread_refs[i], gate_refs[i], mids[i]) for i in range(3)
        ]

        def step(index, carry):
            cols = columns(index)
            blocks = []
            for i in range(3):
                v = by_half(mids[i][:, cols] * invs[i], ga[:, cols], gb[:, cols]).astype(BF16)
                blocks.append(dot(pick_refs[i][...], v))
            g = (gate_d[...] * delta[:, cols].astype(F32)).astype(BF16)
            blocks.append(dot(pick_refs[1][...], g))
            put_rows(outs, blocks, cols)
            return carry

        lax.fori_loop(0, steps_of(width), step, 0)

    (rows2,) = call(
        t2,
        [plain(ret1)]
        + [state(0), kept(0), kept(1), spread(0), spread(2), spread(6), gate(0), gate(2), gate(6)]
        + [pick(1), pick(3), pick(7), state(1), gate(3), gain(1), gain(0)],
        block_shape(4),
        [big, big, big],
        3 * token_flops,
    )
    got2 = exchange(rows2)
    out2, inner_pre = owner(got2, 4, 3, 1, 3, 1, None, (2,), None)
    ret2 = exchange(out2)

    def t3(*refs):
        refs = list(refs)
        take = lambda n: [refs.pop(0) for _ in range(n)]
        rets2 = take(1)[0]
        rets1 = take(1)[0]
        x, spread_x, gate_x, delta, spread_d, pick_n, gate_n, ga, gb = take(9)
        inner = take(1)[0]
        outs = take(1)[0]
        mid, work = take(2)
        add_routes(x, rets1, 1, spread_x, gate_x, mid)
        factor, inv = back_sums(lambda c: mid[:, c], rets2, 1, spread_d, (ga, gb), work)

        def step(index, carry):
            cols = columns(index)
            v = delta[:, cols].astype(F32) + inv * work[:, cols] - mid[:, cols] * factor
            inner[:, cols] = v
            put_rows(outs, [dot(pick_n[...], (gate_n[...] * v).astype(BF16))], cols)
            return carry

        lax.fori_loop(0, steps_of(width), step, 0)

    made3 = call(
        t3,
        [plain(ret2)]
        + [plain(ret1)]
        + [kept(0), spread(2), gate(2), state(1), spread(3), pick(2), gate(2), gain(1), gain(0)],
        [jax.ShapeDtypeStruct(full, F32)] + block_shape(1),
        [big, big],
        2 * token_flops,
    )
    inner0 = made3[0]
    got3 = exchange(made3[1])

    def t3b(*refs):
        refs = list(refs)
        take = lambda n: [refs.pop(0) for _ in range(n)]
        rets2 = take(1)[0]
        rets1 = take(1)[0]
        x, spread_x, gate_x, spread_y, gate_y, pick_n, ga, gb = take(8)
        out_a, out_b, out_rows = take(3)
        mid = take(1)[0]
        add_routes(x, rets1, 0, spread_x, gate_x, mid)

        def finish(index, total):
            cols = columns(index)
            v = mid[:, cols] + gate_y[...] * dot(spread_y[...], block_rows(rets2, 0, cols))
            v = v.astype(BF16)
            out_a[:, cols] = v[:tokens]
            out_b[:, cols] = v[tokens:]
            v = v.astype(F32)
            mid[:, cols] = v
            return total + fold(v * v)

        total = lax.fori_loop(0, steps_of(width), finish, jnp.zeros((pair, 128), F32))
        inv = inverse_rms(total, width)

        def step(index, carry):
            cols = columns(index)
            v = by_half(mid[:, cols] * inv, ga[:, cols], gb[:, cols]).astype(BF16)
            out_rows[:, cols] = dot(pick_n[...], v).astype(BF16)
            return carry

        lax.fori_loop(0, steps_of(width), step, 0)

    half_shape = jax.ShapeDtypeStruct((tokens, width), BF16)
    forward_a, forward_b, next_rows = call(
        t3b,
        [plain(ret2)]
        + [plain(ret1)]
        + [state(0), spread(0), gate(0), spread(1), gate(1), pick(8), plain(gain_above), plain(gain_below)],
        [half_shape, half_shape, jax.ShapeDtypeStruct((64, width), BF16)],
        [big],
        2 * token_flops,
    )
    start_a = lax.ppermute(forward_a, "segment", upward)
    start_b = lax.ppermute(forward_b, "segment", downward)

    out3, _ = owner(got3, 1, 0, 0, 0, None, kept_pre + (0,), (), None)
    ret3 = exchange(out3)
    ret3, start_a, start_b = lax.optimization_barrier((ret3, start_a, start_b))

    def t4(*refs):
        refs = list(refs)
        take = lambda n: [refs.pop(0) for _ in range(n)]
        rets3 = take(1)[0]
        inner, x, spread_x, ga, gb, pick_n, gate_n, rows_f = take(8)
        out_a, out_b, rows_up, rows_down = take(4)
        work = take(1)[0]
        factor, inv = back_sums(lambda c: x[:, c].astype(F32), rets3, 0, spread_x, (ga, gb), work)

        def step(index, carry):
            cols = columns(index)
            v = inner[:, cols] + inv * work[:, cols] - x[:, cols].astype(F32) * factor
            v = v.astype(BF16)
            out_a[:, cols] = v[:tokens]
            out_b[:, cols] = v[tokens:]
            g = (gate_n[...] * v.astype(F32)).astype(BF16)
            blocks = [rows_f[:, cols].astype(F32), dot(pick_n[...], g)]
            put_rows(rows_up, blocks, cols)
            put_rows(rows_down, blocks, cols, rows_up.shape[0])
            return carry

        lax.fori_loop(0, steps_of(width), step, 0)

    next_shape = jax.ShapeDtypeStruct((expert_devices // 2, 2 * CAP, width), BF16)
    back_a, back_b, rows_up, rows_down = call(
        t4,
        [plain(ret3)]
        + [plain(inner0), kept(0), spread(2), gain(0), gain(1), pick(9), gate(9), plain(next_rows)],
        [half_shape, half_shape, next_shape, next_shape],
        [big],
        2 * token_flops,
    )
    from_below = lax.ppermute(rows_up, "segment", upward)
    from_above = lax.ppermute(rows_down, "segment", downward)
    rows4 = jnp.concatenate([from_below, from_above])
    back_a, back_b, rows4 = lax.optimization_barrier((back_a, back_b, rows4))
    got4 = exchange(rows4)
    delta_a = lax.ppermute(back_a, "segment", downward)
    delta_b = lax.ppermute(back_b, "segment", upward)
    out4, _ = owner(got4, 2, 1, 1, 1, None, inner_pre + (0,), (), got1)
    ret4 = exchange(out4)

    def merge(place_ref, start_refs, delta_refs, enter_refs, start, delta):
        bottom = place_ref[0] == 1
        top = place_ref[1] == 1

        def step(index, carry):
            cols = columns(index)
            ef = enter_refs[0][:, cols].astype(F32)
            eg = enter_refs[1][:, cols].astype(F32)
            sa, sb = [r[:, cols].astype(F32) for r in start_refs]
            da, db = [r[:, cols].astype(F32) for r in delta_refs]
            start[:, cols] = jnp.concatenate(
                [jnp.where(bottom, ef[:tokens], sa), jnp.where(top, ef[tokens:], sb)]
            )
            if delta is not None:
                delta[:, cols] = jnp.concatenate(
                    [jnp.where(top, eg[:tokens], da), jnp.where(bottom, eg[tokens:], db)]
                )
            return carry

        lax.fori_loop(0, steps_of(width), step, 0)

    def t5(*refs):
        refs = list(refs)
        take = lambda n: [refs.pop(0) for _ in range(n)]
        place_ref = take(1)[0]
        rets4 = take(1)[0]
        rets1 = take(1)[0]
        starts = take(2)
        deltas = take(2)
        entries = take(2)
        (spread_s, gate_s, pick_s, x, spread_x, gate_x, spread_d, pick_d, gate_d, ga, gb) = take(11)
        middle, inner = take(2)
        outs = take(1)[0]
        mid, work = take(2)
        merge(place_ref, starts, deltas, entries, middle, inner)
        inv_s = add_routes(middle, rets4, 0, spread_s, gate_s, middle)
        add_routes(x, rets1, 2, spread_x, gate_x, mid)
        factor, inv = back_sums(lambda c: mid[:, c], rets4, 1, spread_d, (ga, gb), work)

        def step(index, carry):
            cols = columns(index)
            v = by_half(middle[:, cols] * inv_s, ga[:, cols], gb[:, cols]).astype(BF16)
            d = inner[:, cols] + inv * work[:, cols] - mid[:, cols] * factor
            inner[:, cols] = d
            g = (gate_d[...] * d).astype(BF16)
            put_rows(outs, [dot(pick_s[...], v), dot(pick_d[...], g)], cols)
            return carry

        lax.fori_loop(0, steps_of(width), step, 0)

    made5 = call(
        t5,
        [place_in]
        + [plain(ret4)]
        + [plain(ret1)]
        + each([start_a, start_b, delta_a, delta_b])
        + [enter(0), enter(1)]
        + [spread(4), gate(4), pick(5), kept(1), spread(6), gate(6), spread(7), pick(6), gate(6), gain(1), gain(0)],
        [jax.ShapeDtypeStruct(full, F32), jax.ShapeDtypeStruct(full, F32)] + block_shape(2),
        [big, big],
        4 * token_flops,
    )
    middle1, inner1 = made5[0], made5[1]
    got5 = exchange(made5[2])
    out5, _ = owner(got5, 2, 1, 1, 1, None, kept_pre + (1,), (), None)
    ret5 = exchange(out5)

    def t6(*refs):
        refs = list(refs)
        take = lambda n: [refs.pop(0) for _ in range(n)]
        rets5 = take(1)[0]
        middle, inner, x, spread_s, gate_s, spread_x, ga, gb = take(8)
        out = take(1)[0]
        work = take(1)[0]
        factor, inv = back_sums(lambda c: x[:, c].astype(F32), rets5, 1, spread_x, (ga, gb), work)

        def step(index, carry):
            cols = columns(index)
            f = middle[:, cols] + gate_s[...] * dot(spread_s[...], block_rows(rets5, 0, cols))
            out[:pair, cols] = f.astype(BF16)
            v = inner[:, cols] + inv * work[:, cols] - x[:, cols].astype(F32) * factor
            out[pair:, cols] = v.astype(BF16)
            return carry

        lax.fori_loop(0, steps_of(width), step, 0)

    (result,) = call(
        t6,
        [plain(ret5)]
        + [plain(middle1), plain(inner1), kept(1), spread(5), gate(5), spread(6), gain(0), gain(1)],
        [jax.ShapeDtypeStruct((2 * pair, width), BF16)],
        [big],
        2 * token_flops,
    )
    return result.reshape(state_in.shape)


def solution(mesh):
    in_specs = (
        P("segment", None, ("expert", "dp"), None),
        P(None, None, ("expert", "dp"), None),
        P("segment", None, None, ("expert", "dp"), None),
        P("segment", None, None, None, ("expert", "dp"), None),
        P("segment", None, None, None, ("expert", "dp"), None),
        P("segment", "expert", None, "dp"),
        P("segment", "expert", None, "dp"),
        P("segment", "expert", "dp", None),
        P("segment", None, None),
    )
    out_specs = P("segment", None, ("expert", "dp"), None)
    return jax.shard_map(local, mesh=mesh, in_specs=in_specs, out_specs=out_specs, check_vma=False)
```

```python
import functools

import jax
import jax.numpy as jnp
from jax import lax
from jax.experimental import pallas as pl
from jax.experimental.pallas import tpu as pltpu
from jax.sharding import PartitionSpec as P

CAP = 8
EPSILON = 1e-06
CHUNK = 2048
GROUP = 1
F32 = jnp.float32
BF16 = jnp.bfloat16
NT = (((1,), (1,)), ((), ()))
VMEM_LIMIT = 48 * 1024 * 1024


def dot(a, b):
    return jnp.dot(a, b, preferred_element_type=F32)


def dot_nt(a, b):
    return lax.dot_general(a, b, NT, preferred_element_type=F32)


def whole(shape):
    zeros = (0,) * len(shape)
    return pl.BlockSpec(tuple(shape), lambda i: zeros, memory_space=pltpu.VMEM)


def item(shape, index):
    place = tuple(index) + (0,) * (len(shape) - len(index))
    block = (None,) * len(index) + tuple(shape[len(index):])
    return pl.BlockSpec(block, lambda i: place, memory_space=pltpu.VMEM)


def call(body, operands, out_shapes, scratch, flops, limit=VMEM_LIMIT):
    arrays = [a for a, _ in operands]
    moved = sum(o.size * o.dtype.itemsize for o in out_shapes)
    moved += sum(min(a.size * a.dtype.itemsize, 2**20) for a in arrays)
    return pl.pallas_call(
        body,
        grid=(1,),
        out_shape=out_shapes,
        in_specs=[s for _, s in operands],
        out_specs=[whole(o.shape) for o in out_shapes],
        scratch_shapes=scratch,
        compiler_params=pltpu.CompilerParams(vmem_limit_bytes=limit),
        cost_estimate=pl.CostEstimate(flops=flops, bytes_accessed=moved, transcendentals=0),
    )(*arrays)


def tables_body(place_ref, ids_ref, gates_ref, pick_ref, spread_ref, gate_ref):
    count = ids_ref.shape[0]
    tokens = ids_ref.shape[2]
    half = tokens // 2
    rows = 8 * CAP
    at_bottom = place_ref[0]
    at_top = place_ref[1]
    row = lax.broadcasted_iota(jnp.int32, (rows, tokens), 0)
    lane = lax.broadcasted_iota(jnp.int32, (rows, tokens), 1)
    dest = row >> 3
    slot = (row & 7).astype(F32)
    expert = dest & 3
    dest_sub = dest >> 2
    stream = (lane >= half).astype(jnp.int32)
    t0 = lax.broadcasted_iota(jnp.int32, (tokens, tokens), 0)
    t1 = lax.broadcasted_iota(jnp.int32, (tokens, tokens), 1)
    before = ((t0 < t1) & ((t0 >= half) == (t1 >= half))).astype(F32).astype(BF16)
    end_rows = jnp.where(dest < 4, at_bottom, at_top).astype(F32)

    def step(index, carry):
        order = index & 1
        ids = ids_ref[index]
        gates = gates_ref[index]
        routed = jnp.zeros((rows, tokens), F32)
        weight = jnp.zeros((rows, tokens), F32)
        for k in range(ids.shape[0]):
            hit = ids[k : k + 1, :] == expert
            routed = routed + hit.astype(F32)
            weight = weight + jnp.where(hit, gates[k : k + 1, :], 0.0)
        earlier = dot(routed.astype(BF16), before)
        good = (routed == 1.0) & (earlier == slot) & (dest_sub == (stream ^ order))
        chosen = good.astype(F32)
        weighted = jnp.where(good, weight, 0.0)
        pick_ref[index] = chosen.astype(BF16)
        turned = jnp.transpose(jnp.concatenate([chosen, weighted], axis=0))
        spread_ref[index] = turned[:, :rows].astype(BF16)
        side = lax.broadcasted_iota(jnp.int32, turned.shape, 1)
        gate_ref[index] = jnp.sum(jnp.where(side >= rows, turned, 0.0), axis=1, keepdims=True)
        return carry

    lax.fori_loop(0, count, step, 0)
    for source, target in ((4, count), (7, count + 1)):
        pick_ref[target] = (pick_ref[source].astype(F32) * end_rows).astype(BF16)


def make_tables(place, ids, gates):
    count, _, tokens = ids.shape
    rows = 8 * CAP
    return call(
        tables_body,
        [
            (place, pl.BlockSpec(memory_space=pltpu.SMEM)),
            (ids, whole(ids.shape)),
            (gates, whole(gates.shape)),
        ],
        [
            jax.ShapeDtypeStruct((count + 2, rows, tokens), BF16),
            jax.ShapeDtypeStruct((count, tokens, rows), BF16),
            jax.ShapeDtypeStruct((count, tokens, 1), F32),
        ],
        [],
        10**8,
    )


def by_half(value, first, second):
    half = value.shape[0] // 2
    return jnp.concatenate([value[:half] * first, value[half:] * second], axis=0)


def columns(index):
    return pl.ds(pl.multiple_of(index * CHUNK, CHUNK), CHUNK)


def block_rows(ref, block, cols):
    rows = ref[:, :, cols].astype(F32)[:, block * CAP : (block + 1) * CAP]
    return rows.reshape(ref.shape[0] * CAP, CHUNK).astype(BF16)


def put_rows(out, blocks, cols, first=0):
    for k in range(out.shape[0]):
        start = (first + k) * CAP
        parts = [b[start : start + CAP] for b in blocks]
        rows = parts[0] if len(parts) == 1 else jnp.concatenate(parts, axis=0)
        out[k, :, cols] = rows.astype(BF16)


def fold(value):
    total = value[:, :128]
    for start in range(128, value.shape[1], 128):
        total = total + value[:, start : start + 128]
    return total


def row_total(partial):
    return jnp.sum(partial, axis=-1, keepdims=True)


def inverse_rms(square_partial, width):
    return lax.rsqrt(row_total(square_partial) / width + EPSILON)


def steps_of(width):
    return width // CHUNK


def start_norm(x_ref):
    width = x_ref.shape[1]

    def step(index, total):
        v = x_ref[:, columns(index)].astype(F32)
        return total + fold(v * v)

    total = lax.fori_loop(0, steps_of(width), step, jnp.zeros((x_ref.shape[0], 128), F32))
    return inverse_rms(total, width)


def add_routes(x_ref, ret_refs, block, spread_ref, gate_ref, mid_ref):
    width = x_ref.shape[1]
    spread = spread_ref[...]
    gate = gate_ref[...]

    def step(index, total):
        cols = columns(index)
        m = x_ref[:, cols].astype(F32) + gate * dot(spread, block_rows(ret_refs, block, cols))
        mid_ref[:, cols] = m
        return total + fold(m * m)

    total = lax.fori_loop(0, steps_of(width), step, jnp.zeros((x_ref.shape[0], 128), F32))
    return inverse_rms(total, width)


def back_sums(load, ret_refs, block, spread_ref, gains, work_ref):
    height, width = work_ref.shape
    spread = spread_ref[...]

    def step(index, totals):
        cols = columns(index)
        grad = dot(spread, block_rows(ret_refs, block, cols))
        w = by_half(grad, gains[0][:, cols], gains[1][:, cols])
        work_ref[:, cols] = w
        v = load(cols)
        return (totals[0] + fold(w * v), totals[1] + fold(v * v))

    zero = jnp.zeros((height, 128), F32)
    along, square = lax.fori_loop(0, steps_of(width), step, (zero, zero))
    inv = inverse_rms(square, width)
    return (row_total(along) * (inv * inv * inv) / width, inv)


def owner_call(weights, inputs, picks, pre_blocks, forward_blocks, grad, inner, kept_pre, keep, outs):
    quarters = len(weights) // 2
    width = weights[0].shape[1]
    hidden = weights[0].shape[0] * 2 // 3
    cut = hidden // 2
    sources = inputs[0].shape[0]
    size = sources * CAP
    group = min(GROUP, quarters)
    steps = quarters // group
    span = group * hidden
    blocks = len(picks)
    has_back = grad is not None
    operands = [(a, whole(a.shape)) for a in inputs]
    if kept_pre is not None:
        array_g, array_u, position = kept_pre
        spec = pl.BlockSpec(
            (steps, size, span), lambda i: (0, position, 0), memory_space=pltpu.VMEM
        )
        operands += [(array_g, spec), (array_u, spec)]
    operands += [(w, pl.BlockSpec(memory_space=pl.ANY)) for w in weights]
    shapes = []
    if outs:
        shapes.append(jax.ShapeDtypeStruct((sources, outs * CAP, width), BF16))
    if keep:
        kept_shape = jax.ShapeDtypeStruct((steps, size * len(keep), span), F32)
        shapes += [kept_shape, kept_shape]

    def body(*refs):
        refs = list(refs)
        take = lambda n: [refs.pop(0) for _ in range(n)]
        ins = take(len(inputs))
        pre_g, pre_u = take(2) if kept_pre is not None else (None, None)
        places = take(2 * quarters)
        out_ref = take(1)[0] if outs else None
        keep_g, keep_u = take(2) if keep else (None, None)
        x, wg, wu, wd, acc, sems = refs

        def copies(q, a, b):
            part = lambda ref, start, size: ref.at[pl.ds(start, size)]
            pairs = [
                (part(a, 0, hidden), part(wg, q * hidden, hidden)),
                (part(a, hidden, cut), part(wu, q * hidden, cut)),
                (part(b, 0, cut), part(wu, q * hidden + cut, cut)),
                (part(b, cut, hidden), part(wd, q * hidden, hidden)),
            ]
            if not (forward_blocks or has_back):
                pairs = pairs[:3]
            return [pltpu.make_async_copy(p, t, sems.at[i, q]) for i, (p, t) in enumerate(pairs)]

        for q in range(quarters):
            for copy in copies(q, places[2 * q], places[2 * q + 1]):
                copy.start()

        def load(index, carry):
            cols = columns(index)
            for b, terms in enumerate(picks):
                rows = block_rows(ins[terms[0][0]], terms[0][1], cols)
                for array, block in terms[1:]:
                    rows = rows + block_rows(ins[array], block, cols)
                x[b * size : (b + 1) * size, cols] = rows
            return carry

        lax.fori_loop(0, steps_of(width), load, 0)

        def advance(q):
            for i in range(q * group, (q + 1) * group):
                for copy in copies(i, places[2 * i], places[2 * i + 1]):
                    copy.wait()
            first = q == 0
            part = slice(q * span, (q + 1) * span)
            if pre_blocks:
                rows = x[: pre_blocks * size]
                gate_pre = dot_nt(rows, wg[part])
                up_pre = dot_nt(rows, wu[part])
                for i, b in enumerate(keep):
                    keep_g[q, i * size : (i + 1) * size] = gate_pre[b * size : (b + 1) * size]
                    keep_u[q, i * size : (i + 1) * size] = up_pre[b * size : (b + 1) * size]
            if has_back:
                grad_act = dot_nt(x[grad * size : (grad + 1) * size], wd[part])
            if forward_blocks:
                count = forward_blocks * size
                fg = gate_pre[:count]
                act = (fg * jax.nn.sigmoid(fg) * up_pre[:count]).astype(BF16)
                made = dot(act, wd[part])
                acc[:count] = made if first else acc[:count] + made
            if has_back:
                base = forward_blocks * size
                if kept_pre is not None:
                    bg, bu = pre_g[q], pre_u[q]
                else:
                    bg = gate_pre[inner * size : (inner + 1) * size]
                    bu = up_pre[inner * size : (inner + 1) * size]
                sig = jax.nn.sigmoid(bg)
                grad_gate = (grad_act * bu * sig * (1.0 + bg * (1.0 - sig))).astype(BF16)
                grad_up = (grad_act * bg * sig).astype(BF16)
                made = dot(grad_gate, wg[part]) + dot(grad_up, wu[part])
                acc[base : base + size] = made if first else acc[base : base + size] + made

        for q in range(steps):
            advance(q)

        if outs:

            def store(index, carry):
                cols = columns(index)
                put_rows(out_ref, [acc[b * size : (b + 1) * size, cols] for b in range(outs)], cols)
                return carry

            lax.fori_loop(0, steps_of(width), store, 0)

    held_shape = pltpu.VMEM((quarters * hidden, width), BF16)
    passes = 2 * pre_blocks + forward_blocks + 3 * has_back
    return call(
        body,
        operands,
        shapes,
        [
            pltpu.VMEM((blocks * size, width), BF16),
            held_shape,
            held_shape,
            held_shape,
            pltpu.VMEM((max(outs, 1) * size, width), F32),
            pltpu.SemaphoreType.DMA((4, quarters)),
        ],
        2 * size * width * hidden * quarters * passes,
    )


def t_kept(dp_count, keeps, gain_pair, pick_pair):
    width = keeps[0][0].shape[-1]
    shape = jax.ShapeDtypeStruct((dp_count, 8, len(keeps) * CAP, width), BF16)

    def body(*refs):
        n = len(keeps)
        xs, pick_refs, (ga, gb), out = refs[:n], refs[n : 2 * n], refs[2 * n : 2 * n + 2], refs[-1]
        invs = [start_norm(x) for x in xs]

        def step(index, carry):
            cols = columns(index)
            blocks = []
            for x, inv, p in zip(xs, invs, pick_refs):
                v = by_half(x[:, cols].astype(F32) * inv, ga[:, cols], gb[:, cols]).astype(BF16)
                blocks.append(dot(p[...], v))
            for q in range(dp_count):
                put_rows(out.at[q], blocks, cols)
            return carry

        lax.fori_loop(0, steps_of(width), step, 0)

    return call(body, keeps + pick_pair + gain_pair, [shape], [], 10**8)[0]


def t_early(xs, pick_list, grads, gain_pair):
    width = xs[0][0].shape[-1]
    n, m = len(xs), len(grads)
    shape = jax.ShapeDtypeStruct((8, (n + m) * CAP, width), BF16)

    def body(*refs):
        x_refs, pick_refs = refs[:n], refs[n : 2 * n]
        grad_refs = refs[2 * n : 2 * n + 3 * m]
        ga, gb, out = refs[2 * n + 3 * m :]
        invs = [start_norm(x) for x in x_refs]

        def step(index, carry):
            cols = columns(index)
            blocks = []
            for x, inv, p in zip(x_refs, invs, pick_refs):
                v = by_half(x[:, cols].astype(F32) * inv, ga[:, cols], gb[:, cols]).astype(BF16)
                blocks.append(dot(p[...], v))
            for i in range(m):
                delta, p, gate = grad_refs[3 * i : 3 * i + 3]
                g = (gate[...] * delta[:, cols].astype(F32)).astype(BF16)
                blocks.append(dot(p[...], g))
            put_rows(out, blocks, cols)
            return carry

        lax.fori_loop(0, steps_of(width), step, 0)

    operands = xs + pick_list + [o for g in grads for o in g] + gain_pair
    return call(body, operands, [shape], [], 10**8)[0]


def t_inner(ret, keeps, spread_list, gate_list, pick_list, gain_pair):
    pair, width = keeps[0][0].shape[-2:]
    n = len(keeps)
    full = jax.ShapeDtypeStruct((pair, width), F32)
    shape = jax.ShapeDtypeStruct((8, n * CAP, width), BF16)

    def body(*refs):
        refs = list(refs)
        take = lambda k: [refs.pop(0) for _ in range(k)]
        back = take(1)[0]
        x_refs, spread_refs, gate_refs, pick_refs = take(n), take(n), take(n), take(n)
        ga, gb = take(2)
        mids = take(n)
        out = take(1)[0]
        invs = []
        for i in range(n):
            copies = back.shape[0] // 8
            spread = jnp.concatenate([spread_refs[i][...]] * copies, axis=1)
            gate = gate_refs[i][...]

            def step(index, total, i=i, spread=spread, gate=gate):
                cols = columns(index)
                m = x_refs[i][:, cols].astype(F32) + gate * dot(spread, block_rows(back, i, cols))
                mids[i][:, cols] = m
                return total + fold(m * m)

            total = lax.fori_loop(0, steps_of(width), step, jnp.zeros((pair, 128), F32))
            invs.append(inverse_rms(total, width))

        def step2(index, carry):
            cols = columns(index)
            blocks = []
            for i in range(n):
                v = by_half(mids[i][:, cols] * invs[i], ga[:, cols], gb[:, cols]).astype(BF16)
                blocks.append(dot(pick_refs[i][...], v))
            put_rows(out, blocks, cols)
            return carry

        lax.fori_loop(0, steps_of(width), step2, 0)

    operands = [ret] + keeps + spread_list + gate_list + pick_list + gain_pair
    return call(body, operands, [full] * n + [shape], [], 10**8)


def merge(place_ref, up, down, enter_refs, start, delta):
    tokens = up.shape[0] // 2
    bottom = place_ref[0] == 1
    top = place_ref[1] == 1

    def step(index, carry):
        cols = columns(index)
        ef = enter_refs[0]
        eg = enter_refs[1]
        low = slice(0, tokens)
        high = slice(tokens, 2 * tokens)
        load = lambda r, part: r[part, cols].astype(F32)
        start[low, cols] = jnp.where(bottom, load(ef, low), load(up, low))
        start[high, cols] = jnp.where(top, load(ef, high), load(down, low))
        delta[low, cols] = jnp.where(top, load(eg, low), load(down, high))
        delta[high, cols] = jnp.where(bottom, load(eg, high), load(up, high))
        return carry

    lax.fori_loop(0, steps_of(up.shape[1]), step, 0)


def t_middle(ret, start, delta, forward, backward, gain_pair, place=None, shifts=None, enters=None):
    width = ret[0].shape[-1]
    pair = backward[0][0].shape[-2]
    full = jax.ShapeDtypeStruct((pair, width), F32)
    shape = jax.ShapeDtypeStruct((8, 2 * CAP, width), BF16)
    shifted = place is not None

    def body(*refs):
        refs = list(refs)
        take = lambda k: [refs.pop(0) for _ in range(k)]
        if shifted:
            place_ref, up, down, ef, eg = take(5)
        else:
            start_ref, delta_ref = take(2)
        back = take(1)[0]
        spread_s, gate_s, pick_s, mid, spread_d, pick_d, gate_d, ga, gb = take(9)
        middle, inner, out, work = take(4)
        if shifted:
            merge(place_ref, up, down, (ef, eg), middle, inner)
            start_ref, delta_ref = middle, inner
        inv_s = add_routes(start_ref, back, 0, spread_s, gate_s, middle)
        factor, inv = back_sums(lambda c: mid[:, c], back, 1, spread_d, (ga, gb), work)

        def step(index, carry):
            cols = columns(index)
            v = by_half(middle[:, cols] * inv_s, ga[:, cols], gb[:, cols]).astype(BF16)
            d = delta_ref[:, cols].astype(F32) + inv * work[:, cols] - mid[:, cols] * factor
            inner[:, cols] = d
            g = (gate_d[...] * d).astype(BF16)
            put_rows(out, [dot(pick_s[...], v), dot(pick_d[...], g)], cols)
            return carry

        lax.fori_loop(0, steps_of(width), step, 0)

    first = [place] + shifts + enters if shifted else [start, delta]
    operands = first + [ret] + forward + backward + gain_pair
    return call(body, operands, [full, full, shape], [pltpu.VMEM((pair, width), F32)], 10**8)


def t_next(ret, middle, inner, kept, forward, backward, gain_pair, next_gains):
    width = ret[0].shape[-1]
    pair = kept[0].shape[-2]
    tokens = pair // 2
    ship = jax.ShapeDtypeStruct((pair, width), BF16)
    rows = jax.ShapeDtypeStruct((4, 2 * CAP, width), BF16)

    def body(*refs):
        refs = list(refs)
        take = lambda k: [refs.pop(0) for _ in range(k)]
        back, mid, inn, x = take(4)
        spread_s, gate_s, pick_s, spread_d, pick_d, gate_d, ga, gb, na, nb = take(10)
        up, down, rows_up, rows_down, work, ends = take(6)

        def finish(index, total):
            cols = columns(index)
            v = mid[:, cols] + gate_s[...] * dot(spread_s[...], block_rows(back, 0, cols))
            v = v.astype(BF16)
            up[:tokens, cols] = v[:tokens]
            down[:tokens, cols] = v[tokens:]
            v = v.astype(F32)
            ends[:, cols] = v
            return total + fold(v * v)

        total = lax.fori_loop(0, steps_of(width), finish, jnp.zeros((pair, 128), F32))
        inv_s = inverse_rms(total, width)
        factor, inv = back_sums(
            lambda c: x[:, c].astype(F32), back, 1, spread_d, (ga, gb), work
        )

        def step(index, carry):
            cols = columns(index)
            v = by_half(ends[:, cols] * inv_s, na[:, cols], nb[:, cols]).astype(BF16)
            d = inn[:, cols] + inv * work[:, cols] - x[:, cols].astype(F32) * factor
            d = d.astype(BF16)
            down[tokens:, cols] = d[:tokens]
            up[tokens:, cols] = d[tokens:]
            g = (gate_d[...] * d.astype(F32)).astype(BF16)
            blocks = [dot(pick_s[...], v), dot(pick_d[...], g)]
            put_rows(rows_up, blocks, cols)
            put_rows(rows_down, blocks, cols, rows_up.shape[0])
            return carry

        lax.fori_loop(0, steps_of(width), step, 0)

    big = pltpu.VMEM((pair, width), F32)
    operands = [ret, middle, inner, kept] + forward + backward + gain_pair + next_gains
    return call(body, operands, [ship, ship, rows, rows], [big, big], 10**8)


def t_last(ret, middle, inner, kept, forward, backward, gain_pair):
    width = ret[0].shape[-1]
    pair = kept[0].shape[-2]
    shape = jax.ShapeDtypeStruct((2 * pair, width), BF16)

    def body(*refs):
        refs = list(refs)
        take = lambda k: [refs.pop(0) for _ in range(k)]
        back, mid, inn, x, spread_s, gate_s, spread_d, ga, gb, out, work = refs
        factor, inv = back_sums(
            lambda c: x[:, c].astype(F32), back, 1, spread_d, (ga, gb), work
        )

        def step(index, carry):
            cols = columns(index)
            f = mid[:, cols] + gate_s[...] * dot(spread_s[...], block_rows(back, 0, cols))
            out[:pair, cols] = f.astype(BF16)
            v = inn[:, cols] + inv * work[:, cols] - x[:, cols].astype(F32) * factor
            out[pair:, cols] = v.astype(BF16)
            return carry

        lax.fori_loop(0, steps_of(width), step, 0)

    operands = [ret, middle, inner, kept] + forward + backward + gain_pair
    return call(body, operands, [shape], [pltpu.VMEM((pair, width), F32)], 10**8)[0]


def local(state_in, entering, saved, route_ids, gate_vals, w_gate, w_up, w_down, gains):
    width = state_in.shape[-1]
    tokens = state_in.shape[-2]
    pair = 2 * tokens
    hidden = w_down.shape[-2]
    dp_count = lax.axis_size("dp")
    segment_count = lax.axis_size("segment")
    expert_devices = lax.axis_size("expert")
    section = lax.axis_index("segment").astype(jnp.int32)
    at_bottom = (section == 0).astype(jnp.int32)
    at_top = (section == segment_count - 1).astype(jnp.int32)
    place = jnp.stack([at_bottom, at_top])

    cut = hidden // 2
    turned_up = jnp.transpose(w_up[0, 0])
    own_a = jnp.concatenate([jnp.transpose(w_gate[0, 0]), turned_up[:cut]])
    own_b = jnp.concatenate([turned_up[cut:], w_down[0, 0]])
    ahead = [(i, (i + 1) % dp_count) for i in range(dp_count)]
    behind = [((i + 1) % dp_count, i) for i in range(dp_count)]
    left_a = lax.ppermute(own_a, "dp", ahead)
    right_b = lax.ppermute(own_b, "dp", behind)
    left_b = lax.ppermute(own_b, "dp", ahead)
    right_a = lax.ppermute(own_a, "dp", behind)
    far_a = lax.ppermute(left_a, "dp", ahead)
    far_b = lax.ppermute(right_b, "dp", behind)
    weights = [own_a, own_b, left_a, left_b, right_a, right_b, far_a, far_b]

    def exchange(blocks):
        return lax.all_to_all(blocks, "expert", split_axis=0, concat_axis=0, tiled=True)

    upward = [(i, i + 1) for i in range(segment_count - 1)]
    downward = [(i + 1, i) for i in range(segment_count - 1)]

    def paired(values):
        turned = jnp.transpose(values[0], (0, 1, 4, 2, 3))
        stream_a = turned[:, 0::2]
        stream_b = jnp.flip(turned[:, 1::2], axis=3)
        both = jnp.concatenate([stream_a, stream_b], axis=4)
        both = jnp.transpose(both, (0, 1, 3, 2, 4))
        return both.reshape((8,) + both.shape[3:])

    ids = paired(route_ids).astype(F32)
    gates = paired(gate_vals)
    choices = ids.shape[1]
    gain_rows = gains[0].reshape(2, width // 128, 128)
    pack_down = jnp.concatenate(
        [ids[4, :, :tokens], ids[7, :, tokens:], gates[4, :, :tokens], gates[7, :, tokens:], gain_rows[0]]
    )
    pack_up = jnp.concatenate(
        [ids[7, :, :tokens], ids[4, :, tokens:], gates[7, :, :tokens], gates[4, :, tokens:], gain_rows[1]]
    )
    above = lax.ppermute(pack_down, "segment", downward)
    below = lax.ppermute(pack_up, "segment", upward)
    part = lambda v, i: v[i * choices : (i + 1) * choices]
    more_ids = jnp.stack(
        [
            jnp.concatenate([part(above, 0), part(below, 1)], axis=1),
            jnp.concatenate([part(below, 0), part(above, 1)], axis=1),
        ]
    )
    more_gates = jnp.stack(
        [
            jnp.concatenate([part(above, 2), part(below, 3)], axis=1),
            jnp.concatenate([part(below, 2), part(above, 3)], axis=1),
        ]
    )
    gain_above = above[4 * choices :].reshape(1, width)
    gain_below = below[4 * choices :].reshape(1, width)
    all_ids = jnp.concatenate([ids, more_ids]).astype(jnp.int32)
    all_gates = jnp.concatenate([gates, more_gates])
    picks, spreads, gate_columns = make_tables(place, all_ids, all_gates)

    pick = lambda t: (picks, item(picks.shape, (t,)))
    spread = lambda t: (spreads, item(spreads.shape, (t,)))
    gate = lambda t: (gate_columns, item(gate_columns.shape, (t,)))
    gain_lines = gains[0].reshape(2, 1, width)
    gain = lambda j: (gain_lines, item(gain_lines.shape, (j,)))
    plain = lambda a: (a, whole(a.shape))
    states = state_in.reshape(2, pair, width)
    state = lambda p: (states, item(states.shape, (p,)))
    keeps = saved.reshape(2, pair, width)
    kept = lambda t: (keeps, item(keeps.shape, (t,)))
    enters = entering.reshape(2, pair, width)
    enter = lambda p: (enters, item(enters.shape, (p,)))
    place_in = (place, pl.BlockSpec(memory_space=pltpu.SMEM))
    first_gains = [gain(0), gain(1)]
    second_gains = [gain(1), gain(0)]

    def exchange_all(rows):
        return lax.all_to_all(rows, ("dp", "expert"), split_axis=0, concat_axis=0, tiled=True)

    rows0 = t_kept(dp_count, [kept(0), kept(1)], first_gains, [pick(2), pick(6)])
    got0 = exchange_all(rows0.reshape((dp_count * expert_devices,) + rows0.shape[2:]))
    (out0,) = owner_call(
        weights[:2], [got0], [[(0, 0)], [(0, 1)]], 2, 2, None, None, None, (), 2
    )
    ret0 = exchange_all(out0)

    rows_e = t_early(
        [state(0), kept(0), kept(1), enter(0)],
        [pick(0), pick(2), pick(6), pick(10)],
        [(enter(1), pick(11), gate(7)), (state(1), pick(3), gate(3))],
        first_gains,
    )
    got_e = exchange(rows_e)
    mid_kept0, mid_kept1, rows_i = t_inner(
        plain(ret0),
        [kept(0), kept(1)],
        [spread(2), spread(6)],
        [gate(2), gate(6)],
        [pick(3), pick(7)],
        second_gains,
    )
    got_i = exchange(rows_i)

    (out1,) = owner_call(
        weights, [got_e, got_i], [[(0, 0)], [(1, 0)], [(0, 5)]], 2, 1, 2, 1, None, (), 2
    )
    pre_g, pre_u = owner_call(
        weights, [got_e, got_i], [[(0, 1)], [(0, 2)], [(1, 1)]], 3, 0, None, None, None, (0, 1, 2), 0
    )
    ret1 = exchange(out1)
    middle0, inner0, rows2 = t_middle(
        plain(ret1),
        state(0),
        state(1),
        [spread(0), gate(0), pick(1)],
        [plain(mid_kept0), spread(3), pick(2), gate(2)],
        second_gains,
    )

    got2 = exchange(rows2)
    both = [[(0, 0)], [(0, 1)]]
    (out2,) = owner_call(weights, [got2], both, 1, 1, 1, None, (pre_g, pre_u, 0), (), 2)
    ret2 = exchange(out2)
    ship_up, ship_down, rows_up, rows_down = t_next(
        plain(ret2),
        plain(middle0),
        plain(inner0),
        kept(0),
        [spread(1), gate(1), pick(8)],
        [spread(2), pick(9), gate(9)],
        first_gains,
        [plain(gain_above), plain(gain_below)],
    )

    from_below = lax.ppermute(rows_up, "segment", upward)
    from_above = lax.ppermute(rows_down, "segment", downward)
    rows3 = jnp.concatenate([from_below, from_above])
    ship_up, ship_down, rows3 = lax.optimization_barrier((ship_up, ship_down, rows3))
    shift_up = lax.ppermute(ship_up, "segment", upward)
    shift_down = lax.ppermute(ship_down, "segment", downward)
    got3 = exchange(rows3)
    (out3,) = owner_call(
        weights,
        [got3, got_e],
        [[(0, 0), (1, 3)], [(0, 1), (1, 4)]],
        1,
        1,
        1,
        None,
        (pre_g, pre_u, 2),
        (),
        2,
    )
    ret3 = exchange(out3)
    middle1, inner1, rows4 = t_middle(
        plain(ret3),
        None,
        None,
        [spread(4), gate(4), pick(5)],
        [plain(mid_kept1), spread(7), pick(6), gate(6)],
        second_gains,
        place_in,
        [plain(shift_up), plain(shift_down)],
        [enter(0), enter(1)],
    )

    got4 = exchange(rows4)
    (out4,) = owner_call(weights, [got4], both, 1, 1, 1, None, (pre_g, pre_u, 1), (), 2)
    ret4 = exchange(out4)
    result = t_last(
        plain(ret4),
        plain(middle1),
        plain(inner1),
        kept(1),
        [spread(5), gate(5)],
        [spread(6)],
        first_gains,
    )
    return result.reshape(state_in.shape)


def solution(mesh):
    in_specs = (
        P("segment", None, ("expert", "dp"), None),
        P(None, None, ("expert", "dp"), None),
        P("segment", None, None, ("expert", "dp"), None),
        P("segment", None, None, None, ("expert", "dp"), None),
        P("segment", None, None, None, ("expert", "dp"), None),
        P("segment", "expert", None, "dp"),
        P("segment", "expert", None, "dp"),
        P("segment", "expert", "dp", None),
        P("segment", None, None),
    )
    out_specs = P("segment", None, ("expert", "dp"), None)
    return jax.shard_map(local, mesh=mesh, in_specs=in_specs, out_specs=out_specs, check_vma=False)
```

```python
import functools

import jax
import jax.numpy as jnp
from jax import lax
from jax.experimental import pallas as pl
from jax.experimental.pallas import tpu as pltpu
from jax.sharding import PartitionSpec as P

CAP = 8
EPSILON = 1e-06
CHUNK = 2048
GROUP = 1
F32 = jnp.float32
BF16 = jnp.bfloat16
NT = (((1,), (1,)), ((), ()))
VMEM_LIMIT = 48 * 1024 * 1024


def dot(a, b):
    return jnp.dot(a, b, preferred_element_type=F32)


def dot_nt(a, b):
    return lax.dot_general(a, b, NT, preferred_element_type=F32)


def whole(shape):
    zeros = (0,) * len(shape)
    return pl.BlockSpec(tuple(shape), lambda i: zeros, memory_space=pltpu.VMEM)


def item(shape, index):
    place = tuple(index) + (0,) * (len(shape) - len(index))
    block = (None,) * len(index) + tuple(shape[len(index):])
    return pl.BlockSpec(block, lambda i: place, memory_space=pltpu.VMEM)


def call(body, operands, out_shapes, scratch, flops, limit=VMEM_LIMIT):
    arrays = [a for a, _ in operands]
    moved = sum(o.size * o.dtype.itemsize for o in out_shapes)
    moved += sum(min(a.size * a.dtype.itemsize, 2**20) for a in arrays)
    return pl.pallas_call(
        body,
        grid=(1,),
        out_shape=out_shapes,
        in_specs=[s for _, s in operands],
        out_specs=[whole(o.shape) for o in out_shapes],
        scratch_shapes=scratch,
        compiler_params=pltpu.CompilerParams(vmem_limit_bytes=limit),
        cost_estimate=pl.CostEstimate(flops=flops, bytes_accessed=moved, transcendentals=0),
    )(*arrays)


def tables_body(place_ref, ids_ref, gates_ref, pick_ref, spread_ref, gate_ref):
    count = ids_ref.shape[0]
    tokens = ids_ref.shape[2]
    half = tokens // 2
    rows = 8 * CAP
    at_bottom = place_ref[0]
    at_top = place_ref[1]
    row = lax.broadcasted_iota(jnp.int32, (rows, tokens), 0)
    lane = lax.broadcasted_iota(jnp.int32, (rows, tokens), 1)
    dest = row >> 3
    slot = (row & 7).astype(F32)
    expert = dest & 3
    dest_sub = dest >> 2
    stream = (lane >= half).astype(jnp.int32)
    t0 = lax.broadcasted_iota(jnp.int32, (tokens, tokens), 0)
    t1 = lax.broadcasted_iota(jnp.int32, (tokens, tokens), 1)
    before = ((t0 < t1) & ((t0 >= half) == (t1 >= half))).astype(F32).astype(BF16)
    end_rows = jnp.where(dest < 4, at_bottom, at_top).astype(F32)

    def step(index, carry):
        order = index & 1
        ids = ids_ref[index]
        gates = gates_ref[index]
        routed = jnp.zeros((rows, tokens), F32)
        weight = jnp.zeros((rows, tokens), F32)
        for k in range(ids.shape[0]):
            hit = ids[k : k + 1, :] == expert
            routed = routed + hit.astype(F32)
            weight = weight + jnp.where(hit, gates[k : k + 1, :], 0.0)
        earlier = dot(routed.astype(BF16), before)
        good = (routed == 1.0) & (earlier == slot) & (dest_sub == (stream ^ order))
        chosen = good.astype(F32)
        weighted = jnp.where(good, weight, 0.0)
        pick_ref[index] = chosen.astype(BF16)
        turned = jnp.transpose(jnp.concatenate([chosen, weighted], axis=0))
        spread_ref[index] = turned[:, :rows].astype(BF16)
        side = lax.broadcasted_iota(jnp.int32, turned.shape, 1)
        gate_ref[index] = jnp.sum(jnp.where(side >= rows, turned, 0.0), axis=1, keepdims=True)
        return carry

    lax.fori_loop(0, count, step, 0)
    for source, target in ((4, count), (7, count + 1)):
        pick_ref[target] = (pick_ref[source].astype(F32) * end_rows).astype(BF16)


def make_tables(place, ids, gates):
    count, _, tokens = ids.shape
    rows = 8 * CAP
    return call(
        tables_body,
        [
            (place, pl.BlockSpec(memory_space=pltpu.SMEM)),
            (ids, whole(ids.shape)),
            (gates, whole(gates.shape)),
        ],
        [
            jax.ShapeDtypeStruct((count + 2, rows, tokens), BF16),
            jax.ShapeDtypeStruct((count, tokens, rows), BF16),
            jax.ShapeDtypeStruct((count, tokens, 1), F32),
        ],
        [],
        10**8,
    )


def by_half(value, first, second):
    half = value.shape[0] // 2
    return jnp.concatenate([value[:half] * first, value[half:] * second], axis=0)


def columns(index):
    return pl.ds(pl.multiple_of(index * CHUNK, CHUNK), CHUNK)


def block_rows(ref, block, cols):
    rows = ref[:, :, cols].astype(F32)[:, block * CAP : (block + 1) * CAP]
    return rows.reshape(ref.shape[0] * CAP, CHUNK).astype(BF16)


def put_rows(out, blocks, cols, first=0):
    for k in range(out.shape[0]):
        start = (first + k) * CAP
        parts = [b[start : start + CAP] for b in blocks]
        rows = parts[0] if len(parts) == 1 else jnp.concatenate(parts, axis=0)
        out[k, :, cols] = rows.astype(BF16)


def fold(value):
    total = value[:, :128]
    for start in range(128, value.shape[1], 128):
        total = total + value[:, start : start + 128]
    return total


def row_total(partial):
    return jnp.sum(partial, axis=-1, keepdims=True)


def inverse_rms(square_partial, width):
    return lax.rsqrt(row_total(square_partial) / width + EPSILON)


def steps_of(width):
    return width // CHUNK


def start_norm(x_ref):
    width = x_ref.shape[1]

    def step(index, total):
        v = x_ref[:, columns(index)].astype(F32)
        return total + fold(v * v)

    total = lax.fori_loop(0, steps_of(width), step, jnp.zeros((x_ref.shape[0], 128), F32))
    return inverse_rms(total, width)


def add_routes(x_ref, ret_refs, block, spread_ref, gate_ref, mid_ref):
    width = x_ref.shape[1]
    spread = spread_ref[...]
    gate = gate_ref[...]

    def step(index, total):
        cols = columns(index)
        m = x_ref[:, cols].astype(F32) + gate * dot(spread, block_rows(ret_refs, block, cols))
        mid_ref[:, cols] = m
        return total + fold(m * m)

    total = lax.fori_loop(0, steps_of(width), step, jnp.zeros((x_ref.shape[0], 128), F32))
    return inverse_rms(total, width)


def back_sums(load, ret_refs, block, spread_ref, gains, work_ref):
    height, width = work_ref.shape
    spread = spread_ref[...]

    def step(index, totals):
        cols = columns(index)
        grad = dot(spread, block_rows(ret_refs, block, cols))
        w = by_half(grad, gains[0][:, cols], gains[1][:, cols])
        work_ref[:, cols] = w
        v = load(cols)
        return (totals[0] + fold(w * v), totals[1] + fold(v * v))

    zero = jnp.zeros((height, 128), F32)
    along, square = lax.fori_loop(0, steps_of(width), step, (zero, zero))
    inv = inverse_rms(square, width)
    return (row_total(along) * (inv * inv * inv) / width, inv)


def owner_call(
    weights, inputs, picks, pre_blocks, forward_blocks, grad, inner, kept_pre, keep, outs, so_far=None, partial=False
):
    quarters = len(weights) // 2
    width = weights[0].shape[1]
    hidden = weights[0].shape[0] * 2 // 3
    cut = hidden // 2
    sources = inputs[0].shape[0]
    size = sources * CAP
    group = min(GROUP, quarters)
    steps = quarters // group
    span = group * hidden
    blocks = len(picks)
    has_back = grad is not None
    operands = [(a, whole(a.shape)) for a in inputs]
    if kept_pre is not None:
        array_g, array_u, position = kept_pre
        spec = pl.BlockSpec(
            (steps, size, span), lambda i: (0, position, 0), memory_space=pltpu.VMEM
        )
        operands += [(array_g, spec), (array_u, spec)]
    if so_far is not None:
        operands.append((so_far, whole(so_far.shape)))
    operands += [(w, pl.BlockSpec(memory_space=pl.ANY)) for w in weights]
    shapes = []
    if partial:
        shapes.append(jax.ShapeDtypeStruct((outs * size, width), F32))
    elif outs:
        shapes.append(jax.ShapeDtypeStruct((sources, outs * CAP, width), BF16))
    if keep:
        kept_shape = jax.ShapeDtypeStruct((steps, size * len(keep), span), F32)
        shapes += [kept_shape, kept_shape]

    def body(*refs):
        refs = list(refs)
        take = lambda n: [refs.pop(0) for _ in range(n)]
        ins = take(len(inputs))
        pre_g, pre_u = take(2) if kept_pre is not None else (None, None)
        base_ref = take(1)[0] if so_far is not None else None
        places = take(2 * quarters)
        out_ref = take(1)[0] if outs else None
        keep_g, keep_u = take(2) if keep else (None, None)
        x, wg, wu, wd, acc, sems = refs
        if partial:
            acc = out_ref

        def copies(q, a, b):
            part = lambda ref, start, size: ref.at[pl.ds(start, size)]
            pairs = [
                (part(a, 0, hidden), part(wg, q * hidden, hidden)),
                (part(a, hidden, cut), part(wu, q * hidden, cut)),
                (part(b, 0, cut), part(wu, q * hidden + cut, cut)),
                (part(b, cut, hidden), part(wd, q * hidden, hidden)),
            ]
            if not (forward_blocks or has_back):
                pairs = pairs[:3]
            return [pltpu.make_async_copy(p, t, sems.at[i, q]) for i, (p, t) in enumerate(pairs)]

        for q in range(quarters):
            for copy in copies(q, places[2 * q], places[2 * q + 1]):
                copy.start()

        def load(index, carry):
            cols = columns(index)
            for b, terms in enumerate(picks):
                rows = block_rows(ins[terms[0][0]], terms[0][1], cols)
                for array, block in terms[1:]:
                    rows = rows + block_rows(ins[array], block, cols)
                x[b * size : (b + 1) * size, cols] = rows
            return carry

        lax.fori_loop(0, steps_of(width), load, 0)

        def add(rows, made, first):
            if not first:
                made = acc[rows] + made
            elif so_far is not None:
                made = base_ref[rows] + made
            acc[rows] = made

        def advance(q):
            for i in range(q * group, (q + 1) * group):
                for copy in copies(i, places[2 * i], places[2 * i + 1]):
                    copy.wait()
            first = q == 0
            part = slice(q * span, (q + 1) * span)
            if pre_blocks:
                rows = x[: pre_blocks * size]
                gate_pre = dot_nt(rows, wg[part])
                up_pre = dot_nt(rows, wu[part])
                for i, b in enumerate(keep):
                    keep_g[q, i * size : (i + 1) * size] = gate_pre[b * size : (b + 1) * size]
                    keep_u[q, i * size : (i + 1) * size] = up_pre[b * size : (b + 1) * size]
            if has_back:
                grad_act = dot_nt(x[grad * size : (grad + 1) * size], wd[part])
            if forward_blocks:
                count = forward_blocks * size
                fg = gate_pre[:count]
                act = (fg * jax.nn.sigmoid(fg) * up_pre[:count]).astype(BF16)
                made = dot(act, wd[part])
                add(slice(0, count), made, first)
            if has_back:
                base = forward_blocks * size
                if kept_pre is not None:
                    bg, bu = pre_g[q], pre_u[q]
                else:
                    bg = gate_pre[inner * size : (inner + 1) * size]
                    bu = up_pre[inner * size : (inner + 1) * size]
                sig = jax.nn.sigmoid(bg)
                grad_gate = (grad_act * bu * sig * (1.0 + bg * (1.0 - sig))).astype(BF16)
                grad_up = (grad_act * bg * sig).astype(BF16)
                made = dot(grad_gate, wg[part]) + dot(grad_up, wu[part])
                add(slice(base, base + size), made, first)

        for q in range(steps):
            advance(q)

        if outs and not partial:

            def store(index, carry):
                cols = columns(index)
                put_rows(out_ref, [acc[b * size : (b + 1) * size, cols] for b in range(outs)], cols)
                return carry

            lax.fori_loop(0, steps_of(width), store, 0)

    held_shape = pltpu.VMEM((quarters * hidden, width), BF16)
    passes = 2 * pre_blocks + forward_blocks + 3 * has_back
    return call(
        body,
        operands,
        shapes,
        [
            pltpu.VMEM((blocks * size, width), BF16),
            held_shape,
            held_shape,
            held_shape,
            pltpu.VMEM((max(outs, 1) * size, width), F32),
            pltpu.SemaphoreType.DMA((4, quarters)),
        ],
        2 * size * width * hidden * quarters * passes,
    )


def t_kept(dp_count, keeps, gain_pair, pick_pair):
    width = keeps[0][0].shape[-1]
    shape = jax.ShapeDtypeStruct((dp_count, 8, len(keeps) * CAP, width), BF16)

    def body(*refs):
        n = len(keeps)
        xs, pick_refs, (ga, gb), out = refs[:n], refs[n : 2 * n], refs[2 * n : 2 * n + 2], refs[-1]
        invs = [start_norm(x) for x in xs]

        def step(index, carry):
            cols = columns(index)
            blocks = []
            for x, inv, p in zip(xs, invs, pick_refs):
                v = by_half(x[:, cols].astype(F32) * inv, ga[:, cols], gb[:, cols]).astype(BF16)
                blocks.append(dot(p[...], v))
            for q in range(dp_count):
                put_rows(out.at[q], blocks, cols)
            return carry

        lax.fori_loop(0, steps_of(width), step, 0)

    return call(body, keeps + pick_pair + gain_pair, [shape], [], 10**8)[0]


def t_early(xs, pick_list, grads, gain_pair):
    width = xs[0][0].shape[-1]
    n, m = len(xs), len(grads)
    shape = jax.ShapeDtypeStruct((8, (n + m) * CAP, width), BF16)

    def body(*refs):
        x_refs, pick_refs = refs[:n], refs[n : 2 * n]
        grad_refs = refs[2 * n : 2 * n + 3 * m]
        ga, gb, out = refs[2 * n + 3 * m :]
        invs = [start_norm(x) for x in x_refs]

        def step(index, carry):
            cols = columns(index)
            blocks = []
            for x, inv, p in zip(x_refs, invs, pick_refs):
                v = by_half(x[:, cols].astype(F32) * inv, ga[:, cols], gb[:, cols]).astype(BF16)
                blocks.append(dot(p[...], v))
            for i in range(m):
                delta, p, gate = grad_refs[3 * i : 3 * i + 3]
                g = (gate[...] * delta[:, cols].astype(F32)).astype(BF16)
                blocks.append(dot(p[...], g))
            put_rows(out, blocks, cols)
            return carry

        lax.fori_loop(0, steps_of(width), step, 0)

    operands = xs + pick_list + [o for g in grads for o in g] + gain_pair
    return call(body, operands, [shape], [], 10**8)[0]


def t_inner(ret, keeps, spread_list, gate_list, pick_list, gain_pair):
    pair, width = keeps[0][0].shape[-2:]
    n = len(keeps)
    full = jax.ShapeDtypeStruct((pair, width), F32)
    shape = jax.ShapeDtypeStruct((8, n * CAP, width), BF16)

    def body(*refs):
        refs = list(refs)
        take = lambda k: [refs.pop(0) for _ in range(k)]
        back = take(1)[0]
        x_refs, spread_refs, gate_refs, pick_refs = take(n), take(n), take(n), take(n)
        ga, gb = take(2)
        mids = take(n)
        out = take(1)[0]
        invs = []
        for i in range(n):
            copies = back.shape[0] // 8
            spread = jnp.concatenate([spread_refs[i][...]] * copies, axis=1)
            gate = gate_refs[i][...]

            def step(index, total, i=i, spread=spread, gate=gate):
                cols = columns(index)
                m = x_refs[i][:, cols].astype(F32) + gate * dot(spread, block_rows(back, i, cols))
                mids[i][:, cols] = m
                return total + fold(m * m)

            total = lax.fori_loop(0, steps_of(width), step, jnp.zeros((pair, 128), F32))
            invs.append(inverse_rms(total, width))

        def step2(index, carry):
            cols = columns(index)
            blocks = []
            for i in range(n):
                v = by_half(mids[i][:, cols] * invs[i], ga[:, cols], gb[:, cols]).astype(BF16)
                blocks.append(dot(pick_refs[i][...], v))
            put_rows(out, blocks, cols)
            return carry

        lax.fori_loop(0, steps_of(width), step2, 0)

    operands = [ret] + keeps + spread_list + gate_list + pick_list + gain_pair
    return call(body, operands, [full] * n + [shape], [], 10**8)


def merge(place_ref, up, down, enter_refs, start, delta):
    tokens = up.shape[0] // 2
    bottom = place_ref[0] == 1
    top = place_ref[1] == 1

    def step(index, carry):
        cols = columns(index)
        ef = enter_refs[0]
        eg = enter_refs[1]
        low = slice(0, tokens)
        high = slice(tokens, 2 * tokens)
        load = lambda r, part: r[part, cols].astype(F32)
        start[low, cols] = jnp.where(bottom, load(ef, low), load(up, low))
        start[high, cols] = jnp.where(top, load(ef, high), load(down, low))
        delta[low, cols] = jnp.where(top, load(eg, low), load(down, high))
        delta[high, cols] = jnp.where(bottom, load(eg, high), load(up, high))
        return carry

    lax.fori_loop(0, steps_of(up.shape[1]), step, 0)


def t_middle(ret, start, delta, forward, backward, gain_pair, place=None, shifts=None, enters=None):
    width = ret[0].shape[-1]
    pair = backward[0][0].shape[-2]
    full = jax.ShapeDtypeStruct((pair, width), F32)
    shape = jax.ShapeDtypeStruct((8, 2 * CAP, width), BF16)
    shifted = place is not None

    def body(*refs):
        refs = list(refs)
        take = lambda k: [refs.pop(0) for _ in range(k)]
        if shifted:
            place_ref, up, down, ef, eg = take(5)
        else:
            start_ref, delta_ref = take(2)
        back = take(1)[0]
        spread_s, gate_s, pick_s, mid, spread_d, pick_d, gate_d, ga, gb = take(9)
        middle, inner, out, work = take(4)
        if shifted:
            merge(place_ref, up, down, (ef, eg), middle, inner)
            start_ref, delta_ref = middle, inner
        inv_s = add_routes(start_ref, back, 0, spread_s, gate_s, middle)
        factor, inv = back_sums(lambda c: mid[:, c], back, 1, spread_d, (ga, gb), work)

        def step(index, carry):
            cols = columns(index)
            v = by_half(middle[:, cols] * inv_s, ga[:, cols], gb[:, cols]).astype(BF16)
            d = delta_ref[:, cols].astype(F32) + inv * work[:, cols] - mid[:, cols] * factor
            inner[:, cols] = d
            g = (gate_d[...] * d).astype(BF16)
            put_rows(out, [dot(pick_s[...], v), dot(pick_d[...], g)], cols)
            return carry

        lax.fori_loop(0, steps_of(width), step, 0)

    first = [place] + shifts + enters if shifted else [start, delta]
    operands = first + [ret] + forward + backward + gain_pair
    return call(body, operands, [full, full, shape], [pltpu.VMEM((pair, width), F32)], 10**8)


def t_next(ret, middle, inner, kept, forward, backward, gain_pair, next_gains):
    width = ret[0].shape[-1]
    pair = kept[0].shape[-2]
    tokens = pair // 2
    ship = jax.ShapeDtypeStruct((pair, width), BF16)
    rows = jax.ShapeDtypeStruct((4, 2 * CAP, width), BF16)

    def body(*refs):
        refs = list(refs)
        take = lambda k: [refs.pop(0) for _ in range(k)]
        back, mid, inn, x = take(4)
        spread_s, gate_s, pick_s, spread_d, pick_d, gate_d, ga, gb, na, nb = take(10)
        up, down, rows_up, rows_down, work, ends = take(6)

        def finish(index, total):
            cols = columns(index)
            v = mid[:, cols] + gate_s[...] * dot(spread_s[...], block_rows(back, 0, cols))
            v = v.astype(BF16)
            up[:tokens, cols] = v[:tokens]
            down[:tokens, cols] = v[tokens:]
            v = v.astype(F32)
            ends[:, cols] = v
            return total + fold(v * v)

        total = lax.fori_loop(0, steps_of(width), finish, jnp.zeros((pair, 128), F32))
        inv_s = inverse_rms(total, width)
        factor, inv = back_sums(
            lambda c: x[:, c].astype(F32), back, 1, spread_d, (ga, gb), work
        )

        def step(index, carry):
            cols = columns(index)
            v = by_half(ends[:, cols] * inv_s, na[:, cols], nb[:, cols]).astype(BF16)
            d = inn[:, cols] + inv * work[:, cols] - x[:, cols].astype(F32) * factor
            d = d.astype(BF16)
            down[tokens:, cols] = d[:tokens]
            up[tokens:, cols] = d[tokens:]
            g = (gate_d[...] * d.astype(F32)).astype(BF16)
            blocks = [dot(pick_s[...], v), dot(pick_d[...], g)]
            put_rows(rows_up, blocks, cols)
            put_rows(rows_down, blocks, cols, rows_up.shape[0])
            return carry

        lax.fori_loop(0, steps_of(width), step, 0)

    big = pltpu.VMEM((pair, width), F32)
    operands = [ret, middle, inner, kept] + forward + backward + gain_pair + next_gains
    return call(body, operands, [ship, ship, rows, rows], [big, big], 10**8)


def t_last(ret, middle, inner, kept, forward, backward, gain_pair):
    width = ret[0].shape[-1]
    pair = kept[0].shape[-2]
    shape = jax.ShapeDtypeStruct((2 * pair, width), BF16)

    def body(*refs):
        refs = list(refs)
        take = lambda k: [refs.pop(0) for _ in range(k)]
        back, mid, inn, x, spread_s, gate_s, spread_d, ga, gb, out, work = refs
        factor, inv = back_sums(
            lambda c: x[:, c].astype(F32), back, 1, spread_d, (ga, gb), work
        )

        def step(index, carry):
            cols = columns(index)
            f = mid[:, cols] + gate_s[...] * dot(spread_s[...], block_rows(back, 0, cols))
            out[:pair, cols] = f.astype(BF16)
            v = inn[:, cols] + inv * work[:, cols] - x[:, cols].astype(F32) * factor
            out[pair:, cols] = v.astype(BF16)
            return carry

        lax.fori_loop(0, steps_of(width), step, 0)

    operands = [ret, middle, inner, kept] + forward + backward + gain_pair
    return call(body, operands, [shape], [pltpu.VMEM((pair, width), F32)], 10**8)[0]


def local(state_in, entering, saved, route_ids, gate_vals, w_gate, w_up, w_down, gains):
    width = state_in.shape[-1]
    tokens = state_in.shape[-2]
    pair = 2 * tokens
    hidden = w_down.shape[-2]
    dp_count = lax.axis_size("dp")
    segment_count = lax.axis_size("segment")
    expert_devices = lax.axis_size("expert")
    section = lax.axis_index("segment").astype(jnp.int32)
    at_bottom = (section == 0).astype(jnp.int32)
    at_top = (section == segment_count - 1).astype(jnp.int32)
    place = jnp.stack([at_bottom, at_top])

    cut = hidden // 2
    turned_up = jnp.transpose(w_up[0, 0])
    own_a = jnp.concatenate([jnp.transpose(w_gate[0, 0]), turned_up[:cut]])
    own_b = jnp.concatenate([turned_up[cut:], w_down[0, 0]])
    ahead = [(i, (i + 1) % dp_count) for i in range(dp_count)]
    behind = [((i + 1) % dp_count, i) for i in range(dp_count)]
    left_a = lax.ppermute(own_a, "dp", ahead)
    right_b = lax.ppermute(own_b, "dp", behind)
    left_b = lax.ppermute(own_b, "dp", ahead)
    right_a = lax.ppermute(own_a, "dp", behind)

    def exchange(blocks):
        return lax.all_to_all(blocks, "expert", split_axis=0, concat_axis=0, tiled=True)

    upward = [(i, i + 1) for i in range(segment_count - 1)]
    downward = [(i + 1, i) for i in range(segment_count - 1)]

    def paired(values):
        turned = jnp.transpose(values[0], (0, 1, 4, 2, 3))
        stream_a = turned[:, 0::2]
        stream_b = jnp.flip(turned[:, 1::2], axis=3)
        both = jnp.concatenate([stream_a, stream_b], axis=4)
        both = jnp.transpose(both, (0, 1, 3, 2, 4))
        return both.reshape((8,) + both.shape[3:])

    own_a, own_b, route_ids, gate_vals = lax.optimization_barrier((own_a, own_b, route_ids, gate_vals))
    ids = paired(route_ids).astype(F32)
    gates = paired(gate_vals)
    choices = ids.shape[1]
    gain_rows = gains[0].reshape(2, width // 128, 128)
    pack_down = jnp.concatenate(
        [ids[4, :, :tokens], ids[7, :, tokens:], gates[4, :, :tokens], gates[7, :, tokens:], gain_rows[0]]
    )
    pack_up = jnp.concatenate(
        [ids[7, :, :tokens], ids[4, :, tokens:], gates[7, :, :tokens], gates[4, :, tokens:], gain_rows[1]]
    )
    above = lax.ppermute(pack_down, "segment", downward)
    below = lax.ppermute(pack_up, "segment", upward)
    part = lambda v, i: v[i * choices : (i + 1) * choices]
    more_ids = jnp.stack(
        [
            jnp.concatenate([part(above, 0), part(below, 1)], axis=1),
            jnp.concatenate([part(below, 0), part(above, 1)], axis=1),
        ]
    )
    more_gates = jnp.stack(
        [
            jnp.concatenate([part(above, 2), part(below, 3)], axis=1),
            jnp.concatenate([part(below, 2), part(above, 3)], axis=1),
        ]
    )
    gain_above = above[4 * choices :].reshape(1, width)
    gain_below = below[4 * choices :].reshape(1, width)
    all_ids = jnp.concatenate([ids, more_ids]).astype(jnp.int32)
    all_gates = jnp.concatenate([gates, more_gates])
    picks, spreads, gate_columns = make_tables(place, all_ids, all_gates)

    pick = lambda t: (picks, item(picks.shape, (t,)))
    spread = lambda t: (spreads, item(spreads.shape, (t,)))
    gate = lambda t: (gate_columns, item(gate_columns.shape, (t,)))
    gain_lines = gains[0].reshape(2, 1, width)
    gain = lambda j: (gain_lines, item(gain_lines.shape, (j,)))
    plain = lambda a: (a, whole(a.shape))
    states = state_in.reshape(2, pair, width)
    state = lambda p: (states, item(states.shape, (p,)))
    keeps = saved.reshape(2, pair, width)
    kept = lambda t: (keeps, item(keeps.shape, (t,)))
    enters = entering.reshape(2, pair, width)
    enter = lambda p: (enters, item(enters.shape, (p,)))
    place_in = (place, pl.BlockSpec(memory_space=pltpu.SMEM))
    first_gains = [gain(0), gain(1)]
    second_gains = [gain(1), gain(0)]

    def exchange_all(rows):
        return lax.all_to_all(rows, ("dp", "expert"), split_axis=0, concat_axis=0, tiled=True)

    rows0 = t_kept(dp_count, [kept(0), kept(1)], first_gains, [pick(2), pick(6)])
    got0 = exchange_all(rows0.reshape((dp_count * expert_devices,) + rows0.shape[2:]))
    got0, left_a, right_b = lax.optimization_barrier((got0, left_a, right_b))
    far_a = lax.ppermute(left_a, "dp", ahead)
    far_b = lax.ppermute(right_b, "dp", behind)
    (out0,) = owner_call(
        [own_a, own_b], [got0], [[(0, 0)], [(0, 1)]], 2, 2, None, None, None, (), 2
    )
    ret0 = exchange_all(out0)
    ret0, left_b, right_a = lax.optimization_barrier((ret0, left_b, right_a))
    weights = [own_a, own_b, left_a, left_b, right_a, right_b, far_a, far_b]

    rows_e = t_early(
        [state(0), kept(0), kept(1), enter(0)],
        [pick(0), pick(2), pick(6), pick(10)],
        [(enter(1), pick(11), gate(7)), (state(1), pick(3), gate(3))],
        first_gains,
    )
    got_e = exchange(rows_e)
    mid_kept0, mid_kept1, rows_i = t_inner(
        plain(ret0),
        [kept(0), kept(1)],
        [spread(2), spread(6)],
        [gate(2), gate(6)],
        [pick(3), pick(7)],
        second_gains,
    )
    got_i = exchange(rows_i)

    rows1 = [[(0, 0)], [(1, 0)], [(0, 5)]]
    (near,) = owner_call(
        weights[:-2], [got_e, got_i], rows1, 2, 1, 2, 1, None, (), 2, partial=True
    )
    (out1,) = owner_call(weights[-2:], [got_e, got_i], rows1, 2, 1, 2, 1, None, (), 2, near)
    pre_g, pre_u = owner_call(
        weights, [got_e, got_i], [[(0, 1)], [(0, 2)], [(1, 1)]], 3, 0, None, None, None, (0, 1, 2), 0
    )
    ret1 = exchange(out1)
    middle0, inner0, rows2 = t_middle(
        plain(ret1),
        state(0),
        state(1),
        [spread(0), gate(0), pick(1)],
        [plain(mid_kept0), spread(3), pick(2), gate(2)],
        second_gains,
    )

    got2 = exchange(rows2)
    both = [[(0, 0)], [(0, 1)]]
    (out2,) = owner_call(weights, [got2], both, 1, 1, 1, None, (pre_g, pre_u, 0), (), 2)
    ret2 = exchange(out2)
    ship_up, ship_down, rows_up, rows_down = t_next(
        plain(ret2),
        plain(middle0),
        plain(inner0),
        kept(0),
        [spread(1), gate(1), pick(8)],
        [spread(2), pick(9), gate(9)],
        first_gains,
        [plain(gain_above), plain(gain_below)],
    )

    from_below = lax.ppermute(rows_up, "segment", upward)
    from_above = lax.ppermute(rows_down, "segment", downward)
    rows3 = jnp.concatenate([from_below, from_above])
    ship_up, ship_down, rows3 = lax.optimization_barrier((ship_up, ship_down, rows3))
    shift_up = lax.ppermute(ship_up, "segment", upward)
    shift_down = lax.ppermute(ship_down, "segment", downward)
    got3 = exchange(rows3)
    (out3,) = owner_call(
        weights,
        [got3, got_e],
        [[(0, 0), (1, 3)], [(0, 1), (1, 4)]],
        1,
        1,
        1,
        None,
        (pre_g, pre_u, 2),
        (),
        2,
    )
    ret3 = exchange(out3)
    middle1, inner1, rows4 = t_middle(
        plain(ret3),
        None,
        None,
        [spread(4), gate(4), pick(5)],
        [plain(mid_kept1), spread(7), pick(6), gate(6)],
        second_gains,
        place_in,
        [plain(shift_up), plain(shift_down)],
        [enter(0), enter(1)],
    )

    got4 = exchange(rows4)
    (out4,) = owner_call(weights, [got4], both, 1, 1, 1, None, (pre_g, pre_u, 1), (), 2)
    ret4 = exchange(out4)
    result = t_last(
        plain(ret4),
        plain(middle1),
        plain(inner1),
        kept(1),
        [spread(5), gate(5)],
        [spread(6)],
        first_gains,
    )
    return result.reshape(state_in.shape)


def solution(mesh):
    in_specs = (
        P("segment", None, ("expert", "dp"), None),
        P(None, None, ("expert", "dp"), None),
        P("segment", None, None, ("expert", "dp"), None),
        P("segment", None, None, None, ("expert", "dp"), None),
        P("segment", None, None, None, ("expert", "dp"), None),
        P("segment", "expert", None, "dp"),
        P("segment", "expert", None, "dp"),
        P("segment", "expert", "dp", None),
        P("segment", None, None),
    )
    out_specs = P("segment", None, ("expert", "dp"), None)
    return jax.shard_map(local, mesh=mesh, in_specs=in_specs, out_specs=out_specs, check_vma=False)
```

```python
import functools

import jax
import jax.numpy as jnp
from jax import lax
from jax.experimental import pallas as pl
from jax.experimental.pallas import tpu as pltpu
from jax.sharding import PartitionSpec as P

CAP = 8
EPSILON = 1e-06
CHUNK = 2048
GROUP = 1
F32 = jnp.float32
BF16 = jnp.bfloat16
NT = (((1,), (1,)), ((), ()))
VMEM_LIMIT = 63 * 1024 * 1024


def dot(a, b):
    return jnp.dot(a, b, preferred_element_type=F32)


def dot_nt(a, b):
    return lax.dot_general(a, b, NT, preferred_element_type=F32)


def whole(shape):
    zeros = (0,) * len(shape)
    return pl.BlockSpec(tuple(shape), lambda i: zeros, memory_space=pltpu.VMEM)


def item(shape, index):
    place = tuple(index) + (0,) * (len(shape) - len(index))
    block = (None,) * len(index) + tuple(shape[len(index):])
    return pl.BlockSpec(block, lambda i: place, memory_space=pltpu.VMEM)


def call(body, operands, out_shapes, scratch, flops, limit=VMEM_LIMIT):
    arrays = [a for a, _ in operands]
    moved = sum(o.size * o.dtype.itemsize for o in out_shapes)
    moved += sum(min(a.size * a.dtype.itemsize, 2**20) for a in arrays)
    return pl.pallas_call(
        body,
        grid=(1,),
        out_shape=out_shapes,
        in_specs=[s for _, s in operands],
        out_specs=[whole(o.shape) for o in out_shapes],
        scratch_shapes=scratch,
        compiler_params=pltpu.CompilerParams(vmem_limit_bytes=limit),
        cost_estimate=pl.CostEstimate(flops=flops, bytes_accessed=moved, transcendentals=0),
    )(*arrays)


def tables_body(place_ref, ids_ref, gates_ref, pick_ref, spread_ref, gate_ref):
    count = ids_ref.shape[0]
    tokens = ids_ref.shape[2]
    half = tokens // 2
    rows = 8 * CAP
    at_bottom = place_ref[0]
    at_top = place_ref[1]
    row = lax.broadcasted_iota(jnp.int32, (rows, tokens), 0)
    lane = lax.broadcasted_iota(jnp.int32, (rows, tokens), 1)
    dest = row >> 3
    slot = (row & 7).astype(F32)
    expert = dest & 3
    dest_sub = dest >> 2
    stream = (lane >= half).astype(jnp.int32)
    t0 = lax.broadcasted_iota(jnp.int32, (tokens, tokens), 0)
    t1 = lax.broadcasted_iota(jnp.int32, (tokens, tokens), 1)
    before = ((t0 < t1) & ((t0 >= half) == (t1 >= half))).astype(F32).astype(BF16)
    end_rows = jnp.where(dest < 4, at_bottom, at_top).astype(F32)

    def step(index, carry):
        order = index & 1
        ids = ids_ref[index]
        gates = gates_ref[index]
        routed = jnp.zeros((rows, tokens), F32)
        weight = jnp.zeros((rows, tokens), F32)
        for k in range(ids.shape[0]):
            hit = ids[k : k + 1, :] == expert
            routed = routed + hit.astype(F32)
            weight = weight + jnp.where(hit, gates[k : k + 1, :], 0.0)
        earlier = dot(routed.astype(BF16), before)
        good = (routed == 1.0) & (earlier == slot) & (dest_sub == (stream ^ order))
        chosen = good.astype(F32)
        weighted = jnp.where(good, weight, 0.0)
        pick_ref[index] = chosen.astype(BF16)
        turned = jnp.transpose(jnp.concatenate([chosen, weighted], axis=0))
        spread_ref[index] = turned[:, :rows].astype(BF16)
        side = lax.broadcasted_iota(jnp.int32, turned.shape, 1)
        gate_ref[index] = jnp.sum(jnp.where(side >= rows, turned, 0.0), axis=1, keepdims=True)
        return carry

    lax.fori_loop(0, count, step, 0)
    for source, target in ((4, count), (7, count + 1)):
        pick_ref[target] = (pick_ref[source].astype(F32) * end_rows).astype(BF16)


def make_tables(place, ids, gates):
    count, _, tokens = ids.shape
    rows = 8 * CAP
    return call(
        tables_body,
        [
            (place, pl.BlockSpec(memory_space=pltpu.SMEM)),
            (ids, whole(ids.shape)),
            (gates, whole(gates.shape)),
        ],
        [
            jax.ShapeDtypeStruct((count + 2, rows, tokens), BF16),
            jax.ShapeDtypeStruct((count, tokens, rows), BF16),
            jax.ShapeDtypeStruct((count, tokens, 1), F32),
        ],
        [],
        10**8,
    )


def by_half(value, first, second):
    half = value.shape[0] // 2
    return jnp.concatenate([value[:half] * first, value[half:] * second], axis=0)


def columns(index):
    return pl.ds(pl.multiple_of(index * CHUNK, CHUNK), CHUNK)


def block_rows(ref, block, cols):
    rows = ref[:, :, cols].astype(F32)[:, block * CAP : (block + 1) * CAP]
    return rows.reshape(ref.shape[0] * CAP, CHUNK).astype(BF16)


def put_rows(out, blocks, cols, first=0):
    for k in range(out.shape[0]):
        start = (first + k) * CAP
        parts = [b[start : start + CAP] for b in blocks]
        rows = parts[0] if len(parts) == 1 else jnp.concatenate(parts, axis=0)
        out[k, :, cols] = rows.astype(BF16)


def fold(value):
    total = value[:, :128]
    for start in range(128, value.shape[1], 128):
        total = total + value[:, start : start + 128]
    return total


def row_total(partial):
    return jnp.sum(partial, axis=-1, keepdims=True)


def inverse_rms(square_partial, width):
    return lax.rsqrt(row_total(square_partial) / width + EPSILON)


def steps_of(width):
    return width // CHUNK


def start_norm(x_ref):
    width = x_ref.shape[1]

    def step(index, total):
        v = x_ref[:, columns(index)].astype(F32)
        return total + fold(v * v)

    total = lax.fori_loop(0, steps_of(width), step, jnp.zeros((x_ref.shape[0], 128), F32))
    return inverse_rms(total, width)


def add_routes(x_ref, ret_refs, block, spread_ref, gate_ref, mid_ref):
    width = x_ref.shape[1]
    spread = spread_ref[...]
    gate = gate_ref[...]

    def step(index, total):
        cols = columns(index)
        m = x_ref[:, cols].astype(F32) + gate * dot(spread, block_rows(ret_refs, block, cols))
        mid_ref[:, cols] = m
        return total + fold(m * m)

    total = lax.fori_loop(0, steps_of(width), step, jnp.zeros((x_ref.shape[0], 128), F32))
    return inverse_rms(total, width)


def back_sums(load, ret_refs, block, spread_ref, gains, work_ref):
    height, width = work_ref.shape
    spread = spread_ref[...]

    def step(index, totals):
        cols = columns(index)
        grad = dot(spread, block_rows(ret_refs, block, cols))
        w = by_half(grad, gains[0][:, cols], gains[1][:, cols])
        work_ref[:, cols] = w
        v = load(cols)
        return (totals[0] + fold(w * v), totals[1] + fold(v * v))

    zero = jnp.zeros((height, 128), F32)
    along, square = lax.fori_loop(0, steps_of(width), step, (zero, zero))
    inv = inverse_rms(square, width)
    return (row_total(along) * (inv * inv * inv) / width, inv)


def owner_call(
    weights, inputs, picks, pre_blocks, forward_blocks, grad, inner, kept_pre, keep, outs, so_far=None, partial=False
):
    quarters = len(weights) // 2
    width = weights[0].shape[1]
    hidden = weights[0].shape[0] * 2 // 3
    cut = hidden // 2
    sources = inputs[0].shape[0]
    size = sources * CAP
    group = min(GROUP, quarters)
    steps = quarters // group
    span = group * hidden
    blocks = len(picks)
    has_back = grad is not None
    operands = [(a, whole(a.shape)) for a in inputs]
    if kept_pre is not None:
        array_g, array_u, position = kept_pre
        spec = pl.BlockSpec(
            (steps, size, span), lambda i: (0, position, 0), memory_space=pltpu.VMEM
        )
        operands += [(array_g, spec), (array_u, spec)]
    if so_far is not None:
        operands.append((so_far, whole(so_far.shape)))
    operands += [(w, pl.BlockSpec(memory_space=pl.ANY)) for w in weights]
    shapes = []
    if partial:
        shapes.append(jax.ShapeDtypeStruct((outs * size, width), F32))
    elif outs:
        shapes.append(jax.ShapeDtypeStruct((sources, outs * CAP, width), BF16))
    if keep:
        kept_shape = jax.ShapeDtypeStruct((steps, size * len(keep), span), F32)
        shapes += [kept_shape, kept_shape]

    def body(*refs):
        refs = list(refs)
        take = lambda n: [refs.pop(0) for _ in range(n)]
        ins = take(len(inputs))
        pre_g, pre_u = take(2) if kept_pre is not None else (None, None)
        base_ref = take(1)[0] if so_far is not None else None
        places = take(2 * quarters)
        out_ref = take(1)[0] if outs else None
        keep_g, keep_u = take(2) if keep else (None, None)
        x, wg, wu, wd, acc, sems = refs
        if partial:
            acc = out_ref

        def copies(q, a, b):
            part = lambda ref, start, size: ref.at[pl.ds(start, size)]
            pairs = [
                (part(a, 0, hidden), part(wg, q * hidden, hidden)),
                (part(a, hidden, cut), part(wu, q * hidden, cut)),
                (part(b, 0, cut), part(wu, q * hidden + cut, cut)),
                (part(b, cut, hidden), part(wd, q * hidden, hidden)),
            ]
            if not (forward_blocks or has_back):
                pairs = pairs[:3]
            return [pltpu.make_async_copy(p, t, sems.at[i, q]) for i, (p, t) in enumerate(pairs)]

        for q in range(quarters):
            for copy in copies(q, places[2 * q], places[2 * q + 1]):
                copy.start()

        def load(index, carry):
            cols = columns(index)
            for b, terms in enumerate(picks):
                rows = block_rows(ins[terms[0][0]], terms[0][1], cols)
                for array, block in terms[1:]:
                    rows = rows + block_rows(ins[array], block, cols)
                x[b * size : (b + 1) * size, cols] = rows
            return carry

        lax.fori_loop(0, steps_of(width), load, 0)

        def add(rows, made, first):
            if not first:
                made = acc[rows] + made
            elif so_far is not None:
                made = base_ref[rows] + made
            acc[rows] = made

        def advance(q):
            for i in range(q * group, (q + 1) * group):
                for copy in copies(i, places[2 * i], places[2 * i + 1]):
                    copy.wait()
            first = q == 0
            part = slice(q * span, (q + 1) * span)
            if pre_blocks:
                rows = x[: pre_blocks * size]
                gate_pre = dot_nt(rows, wg[part])
                up_pre = dot_nt(rows, wu[part])
                for i, b in enumerate(keep):
                    keep_g[q, i * size : (i + 1) * size] = gate_pre[b * size : (b + 1) * size]
                    keep_u[q, i * size : (i + 1) * size] = up_pre[b * size : (b + 1) * size]
            if has_back:
                grad_act = dot_nt(x[grad * size : (grad + 1) * size], wd[part])
            if forward_blocks:
                count = forward_blocks * size
                fg = gate_pre[:count]
                act = (fg * jax.nn.sigmoid(fg) * up_pre[:count]).astype(BF16)
                made = dot(act, wd[part])
                add(slice(0, count), made, first)
            if has_back:
                base = forward_blocks * size
                if kept_pre is not None:
                    bg, bu = pre_g[q], pre_u[q]
                else:
                    bg = gate_pre[inner * size : (inner + 1) * size]
                    bu = up_pre[inner * size : (inner + 1) * size]
                sig = jax.nn.sigmoid(bg)
                grad_gate = (grad_act * bu * sig * (1.0 + bg * (1.0 - sig))).astype(BF16)
                grad_up = (grad_act * bg * sig).astype(BF16)
                made = dot(grad_gate, wg[part]) + dot(grad_up, wu[part])
                add(slice(base, base + size), made, first)

        for q in range(steps):
            advance(q)

        if outs and not partial:

            def store(index, carry):
                cols = columns(index)
                put_rows(out_ref, [acc[b * size : (b + 1) * size, cols] for b in range(outs)], cols)
                return carry

            lax.fori_loop(0, steps_of(width), store, 0)

    held_shape = pltpu.VMEM((quarters * hidden, width), BF16)
    passes = 2 * pre_blocks + forward_blocks + 3 * has_back
    return call(
        body,
        operands,
        shapes,
        [
            pltpu.VMEM((blocks * size, width), BF16),
            held_shape,
            held_shape,
            held_shape,
            pltpu.VMEM((max(outs, 1) * size, width), F32),
            pltpu.SemaphoreType.DMA((4, quarters)),
        ],
        2 * size * width * hidden * quarters * passes,
    )


def t_kept(dp_count, keeps, gain_pair, pick_pair):
    width = keeps[0][0].shape[-1]
    shape = jax.ShapeDtypeStruct((dp_count, 8, len(keeps) * CAP, width), BF16)

    def body(*refs):
        n = len(keeps)
        xs, pick_refs, (ga, gb), out = refs[:n], refs[n : 2 * n], refs[2 * n : 2 * n + 2], refs[-1]
        invs = [start_norm(x) for x in xs]

        def step(index, carry):
            cols = columns(index)
            blocks = []
            for x, inv, p in zip(xs, invs, pick_refs):
                v = by_half(x[:, cols].astype(F32) * inv, ga[:, cols], gb[:, cols]).astype(BF16)
                blocks.append(dot(p[...], v))
            for q in range(dp_count):
                put_rows(out.at[q], blocks, cols)
            return carry

        lax.fori_loop(0, steps_of(width), step, 0)

    return call(body, keeps + pick_pair + gain_pair, [shape], [], 10**8)[0]


def t_early(xs, pick_list, grads, gain_pair):
    width = xs[0][0].shape[-1]
    n, m = len(xs), len(grads)
    shape = jax.ShapeDtypeStruct((8, (n + m) * CAP, width), BF16)

    def body(*refs):
        x_refs, pick_refs = refs[:n], refs[n : 2 * n]
        grad_refs = refs[2 * n : 2 * n + 3 * m]
        ga, gb, out = refs[2 * n + 3 * m :]
        invs = [start_norm(x) for x in x_refs]

        def step(index, carry):
            cols = columns(index)
            blocks = []
            for x, inv, p in zip(x_refs, invs, pick_refs):
                v = by_half(x[:, cols].astype(F32) * inv, ga[:, cols], gb[:, cols]).astype(BF16)
                blocks.append(dot(p[...], v))
            for i in range(m):
                delta, p, gate = grad_refs[3 * i : 3 * i + 3]
                g = (gate[...] * delta[:, cols].astype(F32)).astype(BF16)
                blocks.append(dot(p[...], g))
            put_rows(out, blocks, cols)
            return carry

        lax.fori_loop(0, steps_of(width), step, 0)

    operands = xs + pick_list + [o for g in grads for o in g] + gain_pair
    return call(body, operands, [shape], [], 10**8)[0]


def t_inner(ret, keeps, spread_list, gate_list, pick_list, gain_pair):
    pair, width = keeps[0][0].shape[-2:]
    n = len(keeps)
    full = jax.ShapeDtypeStruct((pair, width), F32)
    shape = jax.ShapeDtypeStruct((8, n * CAP, width), BF16)

    def body(*refs):
        refs = list(refs)
        take = lambda k: [refs.pop(0) for _ in range(k)]
        back = take(1)[0]
        x_refs, spread_refs, gate_refs, pick_refs = take(n), take(n), take(n), take(n)
        ga, gb = take(2)
        mids = take(n)
        out = take(1)[0]
        invs = []
        for i in range(n):
            copies = back.shape[0] // 8
            spread = jnp.concatenate([spread_refs[i][...]] * copies, axis=1)
            gate = gate_refs[i][...]

            def step(index, total, i=i, spread=spread, gate=gate):
                cols = columns(index)
                m = x_refs[i][:, cols].astype(F32) + gate * dot(spread, block_rows(back, i, cols))
                mids[i][:, cols] = m
                return total + fold(m * m)

            total = lax.fori_loop(0, steps_of(width), step, jnp.zeros((pair, 128), F32))
            invs.append(inverse_rms(total, width))

        def step2(index, carry):
            cols = columns(index)
            blocks = []
            for i in range(n):
                v = by_half(mids[i][:, cols] * invs[i], ga[:, cols], gb[:, cols]).astype(BF16)
                blocks.append(dot(pick_refs[i][...], v))
            put_rows(out, blocks, cols)
            return carry

        lax.fori_loop(0, steps_of(width), step2, 0)

    operands = [ret] + keeps + spread_list + gate_list + pick_list + gain_pair
    return call(body, operands, [full] * n + [shape], [], 10**8)


def merge(place_ref, up, down, enter_refs, start, delta):
    tokens = up.shape[0] // 2
    bottom = place_ref[0] == 1
    top = place_ref[1] == 1

    def step(index, carry):
        cols = columns(index)
        ef = enter_refs[0]
        eg = enter_refs[1]
        low = slice(0, tokens)
        high = slice(tokens, 2 * tokens)
        load = lambda r, part: r[part, cols].astype(F32)
        start[low, cols] = jnp.where(bottom, load(ef, low), load(up, low))
        start[high, cols] = jnp.where(top, load(ef, high), load(down, low))
        delta[low, cols] = jnp.where(top, load(eg, low), load(down, high))
        delta[high, cols] = jnp.where(bottom, load(eg, high), load(up, high))
        return carry

    lax.fori_loop(0, steps_of(up.shape[1]), step, 0)


def t_middle(ret, start, delta, forward, backward, gain_pair, place=None, shifts=None, enters=None):
    width = ret[0].shape[-1]
    pair = backward[0][0].shape[-2]
    full = jax.ShapeDtypeStruct((pair, width), F32)
    shape = jax.ShapeDtypeStruct((8, 2 * CAP, width), BF16)
    shifted = place is not None

    def body(*refs):
        refs = list(refs)
        take = lambda k: [refs.pop(0) for _ in range(k)]
        if shifted:
            place_ref, up, down, ef, eg = take(5)
        else:
            start_ref, delta_ref = take(2)
        back = take(1)[0]
        spread_s, gate_s, pick_s, mid, spread_d, pick_d, gate_d, ga, gb = take(9)
        middle, inner, out, work = take(4)
        if shifted:
            merge(place_ref, up, down, (ef, eg), middle, inner)
            start_ref, delta_ref = middle, inner
        inv_s = add_routes(start_ref, back, 0, spread_s, gate_s, middle)
        factor, inv = back_sums(lambda c: mid[:, c], back, 1, spread_d, (ga, gb), work)

        def step(index, carry):
            cols = columns(index)
            v = by_half(middle[:, cols] * inv_s, ga[:, cols], gb[:, cols]).astype(BF16)
            d = delta_ref[:, cols].astype(F32) + inv * work[:, cols] - mid[:, cols] * factor
            inner[:, cols] = d
            g = (gate_d[...] * d).astype(BF16)
            put_rows(out, [dot(pick_s[...], v), dot(pick_d[...], g)], cols)
            return carry

        lax.fori_loop(0, steps_of(width), step, 0)

    first = [place] + shifts + enters if shifted else [start, delta]
    operands = first + [ret] + forward + backward + gain_pair
    return call(body, operands, [full, full, shape], [pltpu.VMEM((pair, width), F32)], 10**8)


def t_next(ret, middle, inner, kept, forward, backward, gain_pair, next_gains):
    width = ret[0].shape[-1]
    pair = kept[0].shape[-2]
    tokens = pair // 2
    ship = jax.ShapeDtypeStruct((pair, width), BF16)
    rows = jax.ShapeDtypeStruct((4, 2 * CAP, width), BF16)

    def body(*refs):
        refs = list(refs)
        take = lambda k: [refs.pop(0) for _ in range(k)]
        back, mid, inn, x = take(4)
        spread_s, gate_s, pick_s, spread_d, pick_d, gate_d, ga, gb, na, nb = take(10)
        up, down, rows_up, rows_down, work, ends = take(6)

        def finish(index, total):
            cols = columns(index)
            v = mid[:, cols] + gate_s[...] * dot(spread_s[...], block_rows(back, 0, cols))
            v = v.astype(BF16)
            up[:tokens, cols] = v[:tokens]
            down[:tokens, cols] = v[tokens:]
            v = v.astype(F32)
            ends[:, cols] = v
            return total + fold(v * v)

        total = lax.fori_loop(0, steps_of(width), finish, jnp.zeros((pair, 128), F32))
        inv_s = inverse_rms(total, width)
        factor, inv = back_sums(
            lambda c: x[:, c].astype(F32), back, 1, spread_d, (ga, gb), work
        )

        def step(index, carry):
            cols = columns(index)
            v = by_half(ends[:, cols] * inv_s, na[:, cols], nb[:, cols]).astype(BF16)
            d = inn[:, cols] + inv * work[:, cols] - x[:, cols].astype(F32) * factor
            d = d.astype(BF16)
            down[tokens:, cols] = d[:tokens]
            up[tokens:, cols] = d[tokens:]
            g = (gate_d[...] * d.astype(F32)).astype(BF16)
            blocks = [dot(pick_s[...], v), dot(pick_d[...], g)]
            put_rows(rows_up, blocks, cols)
            put_rows(rows_down, blocks, cols, rows_up.shape[0])
            return carry

        lax.fori_loop(0, steps_of(width), step, 0)

    big = pltpu.VMEM((pair, width), F32)
    operands = [ret, middle, inner, kept] + forward + backward + gain_pair + next_gains
    return call(body, operands, [ship, ship, rows, rows], [big, big], 10**8)


def t_last(ret, middle, inner, kept, forward, backward, gain_pair):
    width = ret[0].shape[-1]
    pair = kept[0].shape[-2]
    shape = jax.ShapeDtypeStruct((2 * pair, width), BF16)

    def body(*refs):
        refs = list(refs)
        take = lambda k: [refs.pop(0) for _ in range(k)]
        back, mid, inn, x, spread_s, gate_s, spread_d, ga, gb, out, work = refs
        factor, inv = back_sums(
            lambda c: x[:, c].astype(F32), back, 1, spread_d, (ga, gb), work
        )

        def step(index, carry):
            cols = columns(index)
            f = mid[:, cols] + gate_s[...] * dot(spread_s[...], block_rows(back, 0, cols))
            out[:pair, cols] = f.astype(BF16)
            v = inn[:, cols] + inv * work[:, cols] - x[:, cols].astype(F32) * factor
            out[pair:, cols] = v.astype(BF16)
            return carry

        lax.fori_loop(0, steps_of(width), step, 0)

    operands = [ret, middle, inner, kept] + forward + backward + gain_pair
    return call(body, operands, [shape], [pltpu.VMEM((pair, width), F32)], 10**8)[0]


def local(state_in, entering, saved, route_ids, gate_vals, w_gate, w_up, w_down, gains):
    width = state_in.shape[-1]
    tokens = state_in.shape[-2]
    pair = 2 * tokens
    hidden = w_down.shape[-2]
    dp_count = lax.axis_size("dp")
    segment_count = lax.axis_size("segment")
    expert_devices = lax.axis_size("expert")
    section = lax.axis_index("segment").astype(jnp.int32)
    at_bottom = (section == 0).astype(jnp.int32)
    at_top = (section == segment_count - 1).astype(jnp.int32)
    place = jnp.stack([at_bottom, at_top])

    cut = hidden // 2
    turned_up = jnp.transpose(w_up[0, 0])
    own_a = jnp.concatenate([jnp.transpose(w_gate[0, 0]), turned_up[:cut]])
    own_b = jnp.concatenate([turned_up[cut:], w_down[0, 0]])
    ahead = [(i, (i + 1) % dp_count) for i in range(dp_count)]
    behind = [((i + 1) % dp_count, i) for i in range(dp_count)]
    left_a = lax.ppermute(own_a, "dp", ahead)
    right_b = lax.ppermute(own_b, "dp", behind)
    left_b = lax.ppermute(own_b, "dp", ahead)
    right_a = lax.ppermute(own_a, "dp", behind)

    def exchange(blocks):
        return lax.all_to_all(blocks, "expert", split_axis=0, concat_axis=0, tiled=True)

    upward = [(i, i + 1) for i in range(segment_count - 1)]
    downward = [(i + 1, i) for i in range(segment_count - 1)]

    def paired(values):
        turned = jnp.transpose(values[0], (0, 1, 4, 2, 3))
        stream_a = turned[:, 0::2]
        stream_b = jnp.flip(turned[:, 1::2], axis=3)
        both = jnp.concatenate([stream_a, stream_b], axis=4)
        both = jnp.transpose(both, (0, 1, 3, 2, 4))
        return both.reshape((8,) + both.shape[3:])

    own_a, own_b, route_ids, gate_vals = lax.optimization_barrier((own_a, own_b, route_ids, gate_vals))
    ids = paired(route_ids).astype(F32)
    gates = paired(gate_vals)
    choices = ids.shape[1]
    gain_rows = gains[0].reshape(2, width // 128, 128)
    pack_down = jnp.concatenate(
        [ids[4, :, :tokens], ids[7, :, tokens:], gates[4, :, :tokens], gates[7, :, tokens:], gain_rows[0]]
    )
    pack_up = jnp.concatenate(
        [ids[7, :, :tokens], ids[4, :, tokens:], gates[7, :, :tokens], gates[4, :, tokens:], gain_rows[1]]
    )
    above = lax.ppermute(pack_down, "segment", downward)
    below = lax.ppermute(pack_up, "segment", upward)
    part = lambda v, i: v[i * choices : (i + 1) * choices]
    more_ids = jnp.stack(
        [
            jnp.concatenate([part(above, 0), part(below, 1)], axis=1),
            jnp.concatenate([part(below, 0), part(above, 1)], axis=1),
        ]
    )
    more_gates = jnp.stack(
        [
            jnp.concatenate([part(above, 2), part(below, 3)], axis=1),
            jnp.concatenate([part(below, 2), part(above, 3)], axis=1),
        ]
    )
    gain_above = above[4 * choices :].reshape(1, width)
    gain_below = below[4 * choices :].reshape(1, width)
    all_ids = jnp.concatenate([ids, more_ids]).astype(jnp.int32)
    all_gates = jnp.concatenate([gates, more_gates])
    picks, spreads, gate_columns = make_tables(place, all_ids, all_gates)

    pick = lambda t: (picks, item(picks.shape, (t,)))
    spread = lambda t: (spreads, item(spreads.shape, (t,)))
    gate = lambda t: (gate_columns, item(gate_columns.shape, (t,)))
    gain_lines = gains[0].reshape(2, 1, width)
    gain = lambda j: (gain_lines, item(gain_lines.shape, (j,)))
    plain = lambda a: (a, whole(a.shape))
    states = state_in.reshape(2, pair, width)
    state = lambda p: (states, item(states.shape, (p,)))
    keeps = saved.reshape(2, pair, width)
    kept = lambda t: (keeps, item(keeps.shape, (t,)))
    enters = entering.reshape(2, pair, width)
    enter = lambda p: (enters, item(enters.shape, (p,)))
    place_in = (place, pl.BlockSpec(memory_space=pltpu.SMEM))
    first_gains = [gain(0), gain(1)]
    second_gains = [gain(1), gain(0)]

    def exchange_all(rows):
        return lax.all_to_all(rows, ("dp", "expert"), split_axis=0, concat_axis=0, tiled=True)

    rows0 = t_kept(dp_count, [kept(0), kept(1)], first_gains, [pick(2), pick(6)])
    got0 = exchange_all(rows0.reshape((dp_count * expert_devices,) + rows0.shape[2:]))
    got0, left_a, right_b = lax.optimization_barrier((got0, left_a, right_b))
    far_a = lax.ppermute(left_a, "dp", ahead)
    far_b = lax.ppermute(right_b, "dp", behind)
    (out0,) = owner_call(
        [own_a, own_b], [got0], [[(0, 0)], [(0, 1)]], 2, 2, None, None, None, (), 2
    )
    ret0 = exchange_all(out0)
    late_states, left_b, right_a = lax.optimization_barrier((states, left_b, right_a))
    weights = [own_a, own_b, left_a, left_b, right_a, right_b, far_a, far_b]

    rows_e = t_early(
        [(late_states, item(states.shape, (0,))), kept(0), kept(1), enter(0)],
        [pick(0), pick(2), pick(6), pick(10)],
        [(enter(1), pick(11), gate(7)), (state(1), pick(3), gate(3))],
        first_gains,
    )
    got_e = exchange(rows_e)
    mid_kept0, mid_kept1, rows_i = t_inner(
        plain(ret0),
        [kept(0), kept(1)],
        [spread(2), spread(6)],
        [gate(2), gate(6)],
        [pick(3), pick(7)],
        second_gains,
    )
    got_i = exchange(rows_i)

    rows1 = [[(0, 0)], [(1, 0)], [(0, 5)]]
    (near,) = owner_call(
        weights[:-2], [got_e, got_i], rows1, 2, 1, 2, 1, None, (), 2, partial=True
    )
    (out1,) = owner_call(weights[-2:], [got_e, got_i], rows1, 2, 1, 2, 1, None, (), 2, near)
    pre_g, pre_u = owner_call(
        weights, [got_e, got_i], [[(0, 1)], [(0, 2)], [(1, 1)]], 3, 0, None, None, None, (0, 1, 2), 0
    )
    ret1 = exchange(out1)
    middle0, inner0, rows2 = t_middle(
        plain(ret1),
        state(0),
        state(1),
        [spread(0), gate(0), pick(1)],
        [plain(mid_kept0), spread(3), pick(2), gate(2)],
        second_gains,
    )

    got2 = exchange(rows2)
    both = [[(0, 0)], [(0, 1)]]
    (out2,) = owner_call(weights, [got2], both, 1, 1, 1, None, (pre_g, pre_u, 0), (), 2)
    ret2 = exchange(out2)
    ship_up, ship_down, rows_up, rows_down = t_next(
        plain(ret2),
        plain(middle0),
        plain(inner0),
        kept(0),
        [spread(1), gate(1), pick(8)],
        [spread(2), pick(9), gate(9)],
        first_gains,
        [plain(gain_above), plain(gain_below)],
    )

    from_below = lax.ppermute(rows_up, "segment", upward)
    from_above = lax.ppermute(rows_down, "segment", downward)
    rows3 = jnp.concatenate([from_below, from_above])
    ship_up, ship_down, rows3 = lax.optimization_barrier((ship_up, ship_down, rows3))
    shift_up = lax.ppermute(ship_up, "segment", upward)
    shift_down = lax.ppermute(ship_down, "segment", downward)
    got3 = exchange(rows3)
    (out3,) = owner_call(
        weights,
        [got3, got_e],
        [[(0, 0), (1, 3)], [(0, 1), (1, 4)]],
        1,
        1,
        1,
        None,
        (pre_g, pre_u, 2),
        (),
        2,
    )
    ret3 = exchange(out3)
    middle1, inner1, rows4 = t_middle(
        plain(ret3),
        None,
        None,
        [spread(4), gate(4), pick(5)],
        [plain(mid_kept1), spread(7), pick(6), gate(6)],
        second_gains,
        place_in,
        [plain(shift_up), plain(shift_down)],
        [enter(0), enter(1)],
    )

    got4 = exchange(rows4)
    (out4,) = owner_call(weights, [got4], both, 1, 1, 1, None, (pre_g, pre_u, 1), (), 2)
    ret4 = exchange(out4)
    result = t_last(
        plain(ret4),
        plain(middle1),
        plain(inner1),
        kept(1),
        [spread(5), gate(5)],
        [spread(6)],
        first_gains,
    )
    return result.reshape(state_in.shape)


def solution(mesh):
    in_specs = (
        P("segment", None, ("expert", "dp"), None),
        P(None, None, ("expert", "dp"), None),
        P("segment", None, None, ("expert", "dp"), None),
        P("segment", None, None, None, ("expert", "dp"), None),
        P("segment", None, None, None, ("expert", "dp"), None),
        P("segment", "expert", None, "dp"),
        P("segment", "expert", None, "dp"),
        P("segment", "expert", "dp", None),
        P("segment", None, None),
    )
    out_specs = P("segment", None, ("expert", "dp"), None)
    return jax.shard_map(local, mesh=mesh, in_specs=in_specs, out_specs=out_specs, check_vma=False)
```

```python
import functools

import jax
import jax.numpy as jnp
from jax import lax
from jax.experimental import pallas as pl
from jax.experimental.pallas import tpu as pltpu
from jax.sharding import PartitionSpec as P

CAP = 8
EPSILON = 1e-06
CHUNK = 2048
GROUP = 1
F32 = jnp.float32
BF16 = jnp.bfloat16
NT = (((1,), (1,)), ((), ()))
VMEM_LIMIT = 48 * 1024 * 1024


def dot(a, b):
    return jnp.dot(a, b, preferred_element_type=F32)


def dot_nt(a, b):
    return lax.dot_general(a, b, NT, preferred_element_type=F32)


def whole(shape):
    zeros = (0,) * len(shape)
    return pl.BlockSpec(tuple(shape), lambda i: zeros, memory_space=pltpu.VMEM)


def item(shape, index):
    place = tuple(index) + (0,) * (len(shape) - len(index))
    block = (None,) * len(index) + tuple(shape[len(index):])
    return pl.BlockSpec(block, lambda i: place, memory_space=pltpu.VMEM)


def call(body, operands, out_shapes, scratch, flops, limit=VMEM_LIMIT):
    arrays = [a for a, _ in operands]
    moved = sum(o.size * o.dtype.itemsize for o in out_shapes)
    moved += sum(min(a.size * a.dtype.itemsize, 2**20) for a in arrays)
    return pl.pallas_call(
        body,
        grid=(1,),
        out_shape=out_shapes,
        in_specs=[s for _, s in operands],
        out_specs=[whole(o.shape) for o in out_shapes],
        scratch_shapes=scratch,
        compiler_params=pltpu.CompilerParams(vmem_limit_bytes=limit),
        cost_estimate=pl.CostEstimate(flops=flops, bytes_accessed=moved, transcendentals=0),
    )(*arrays)


def tables_body(place_ref, ids_ref, gates_ref, pick_ref, spread_ref, gate_ref):
    count = ids_ref.shape[0]
    tokens = ids_ref.shape[2]
    half = tokens // 2
    rows = 8 * CAP
    at_bottom = place_ref[0]
    at_top = place_ref[1]
    row = lax.broadcasted_iota(jnp.int32, (rows, tokens), 0)
    lane = lax.broadcasted_iota(jnp.int32, (rows, tokens), 1)
    dest = row >> 3
    slot = (row & 7).astype(F32)
    expert = dest & 3
    dest_sub = dest >> 2
    stream = (lane >= half).astype(jnp.int32)
    t0 = lax.broadcasted_iota(jnp.int32, (tokens, tokens), 0)
    t1 = lax.broadcasted_iota(jnp.int32, (tokens, tokens), 1)
    before = ((t0 < t1) & ((t0 >= half) == (t1 >= half))).astype(F32).astype(BF16)
    end_rows = jnp.where(dest < 4, at_bottom, at_top).astype(F32)

    def step(index, carry):
        order = index & 1
        ids = ids_ref[index]
        gates = gates_ref[index]
        routed = jnp.zeros((rows, tokens), F32)
        weight = jnp.zeros((rows, tokens), F32)
        for k in range(ids.shape[0]):
            hit = ids[k : k + 1, :] == expert
            routed = routed + hit.astype(F32)
            weight = weight + jnp.where(hit, gates[k : k + 1, :], 0.0)
        earlier = dot(routed.astype(BF16), before)
        good = (routed == 1.0) & (earlier == slot) & (dest_sub == (stream ^ order))
        chosen = good.astype(F32)
        weighted = jnp.where(good, weight, 0.0)
        pick_ref[index] = chosen.astype(BF16)
        turned = jnp.transpose(jnp.concatenate([chosen, weighted], axis=0))
        spread_ref[index] = turned[:, :rows].astype(BF16)
        side = lax.broadcasted_iota(jnp.int32, turned.shape, 1)
        gate_ref[index] = jnp.sum(jnp.where(side >= rows, turned, 0.0), axis=1, keepdims=True)
        return carry

    lax.fori_loop(0, count, step, 0)
    for source, target in ((4, count), (7, count + 1)):
        pick_ref[target] = (pick_ref[source].astype(F32) * end_rows).astype(BF16)


def make_tables(place, ids, gates):
    count, _, tokens = ids.shape
    rows = 8 * CAP
    return call(
        tables_body,
        [
            (place, pl.BlockSpec(memory_space=pltpu.SMEM)),
            (ids, whole(ids.shape)),
            (gates, whole(gates.shape)),
        ],
        [
            jax.ShapeDtypeStruct((count + 2, rows, tokens), BF16),
            jax.ShapeDtypeStruct((count, tokens, rows), BF16),
            jax.ShapeDtypeStruct((count, tokens, 1), F32),
        ],
        [],
        10**8,
    )


def by_half(value, first, second):
    half = value.shape[0] // 2
    return jnp.concatenate([value[:half] * first, value[half:] * second], axis=0)


def columns(index):
    return pl.ds(pl.multiple_of(index * CHUNK, CHUNK), CHUNK)


def block_rows(ref, block, cols):
    rows = ref[:, :, cols].astype(F32)[:, block * CAP : (block + 1) * CAP]
    return rows.reshape(ref.shape[0] * CAP, CHUNK).astype(BF16)


def put_rows(out, blocks, cols, first=0):
    for k in range(out.shape[0]):
        start = (first + k) * CAP
        parts = [b[start : start + CAP] for b in blocks]
        rows = parts[0] if len(parts) == 1 else jnp.concatenate(parts, axis=0)
        out[k, :, cols] = rows.astype(BF16)


def fold(value):
    total = value[:, :128]
    for start in range(128, value.shape[1], 128):
        total = total + value[:, start : start + 128]
    return total


def row_total(partial):
    return jnp.sum(partial, axis=-1, keepdims=True)


def inverse_rms(square_partial, width):
    return lax.rsqrt(row_total(square_partial) / width + EPSILON)


def steps_of(width):
    return width // CHUNK


def start_norm(x_ref):
    width = x_ref.shape[1]

    def step(index, total):
        v = x_ref[:, columns(index)].astype(F32)
        return total + fold(v * v)

    total = lax.fori_loop(0, steps_of(width), step, jnp.zeros((x_ref.shape[0], 128), F32))
    return inverse_rms(total, width)


def add_routes(x_ref, ret_refs, block, spread_ref, gate_ref, mid_ref):
    width = x_ref.shape[1]
    spread = spread_ref[...]
    gate = gate_ref[...]

    def step(index, total):
        cols = columns(index)
        m = x_ref[:, cols].astype(F32) + gate * dot(spread, block_rows(ret_refs, block, cols))
        mid_ref[:, cols] = m
        return total + fold(m * m)

    total = lax.fori_loop(0, steps_of(width), step, jnp.zeros((x_ref.shape[0], 128), F32))
    return inverse_rms(total, width)


def back_sums(load, ret_refs, block, spread_ref, gains, work_ref):
    height, width = work_ref.shape
    spread = spread_ref[...]

    def step(index, totals):
        cols = columns(index)
        grad = dot(spread, block_rows(ret_refs, block, cols))
        w = by_half(grad, gains[0][:, cols], gains[1][:, cols])
        work_ref[:, cols] = w
        v = load(cols)
        return (totals[0] + fold(w * v), totals[1] + fold(v * v))

    zero = jnp.zeros((height, 128), F32)
    along, square = lax.fori_loop(0, steps_of(width), step, (zero, zero))
    inv = inverse_rms(square, width)
    return (row_total(along) * (inv * inv * inv) / width, inv)


def owner_call(
    weights, inputs, picks, pre_blocks, forward_blocks, grad, inner, kept_pre, keep, outs, so_far=None, partial=False
):
    quarters = len(weights) // 2
    width = weights[0].shape[1]
    hidden = weights[0].shape[0] * 2 // 3
    cut = hidden // 2
    sources = inputs[0].shape[0]
    size = sources * CAP
    group = min(GROUP, quarters)
    steps = quarters // group
    span = group * hidden
    blocks = len(picks)
    has_back = grad is not None
    operands = [(a, whole(a.shape)) for a in inputs]
    if kept_pre is not None:
        array_g, array_u, position = kept_pre
        spec = pl.BlockSpec(
            (steps, size, span), lambda i: (0, position, 0), memory_space=pltpu.VMEM
        )
        operands += [(array_g, spec), (array_u, spec)]
    if so_far is not None:
        operands.append((so_far, whole(so_far.shape)))
    operands += [(w, pl.BlockSpec(memory_space=pl.ANY)) for w in weights]
    shapes = []
    if partial:
        shapes.append(jax.ShapeDtypeStruct((outs * size, width), F32))
    elif outs:
        shapes.append(jax.ShapeDtypeStruct((sources, outs * CAP, width), BF16))
    if keep:
        kept_shape = jax.ShapeDtypeStruct((steps, size * len(keep), span), F32)
        shapes += [kept_shape, kept_shape]

    def body(*refs):
        refs = list(refs)
        take = lambda n: [refs.pop(0) for _ in range(n)]
        ins = take(len(inputs))
        pre_g, pre_u = take(2) if kept_pre is not None else (None, None)
        base_ref = take(1)[0] if so_far is not None else None
        places = take(2 * quarters)
        out_ref = take(1)[0] if outs else None
        keep_g, keep_u = take(2) if keep else (None, None)
        x, wg, wu, wd, acc, sems = refs
        if partial:
            acc = out_ref

        def copies(q, a, b):
            part = lambda ref, start, size: ref.at[pl.ds(start, size)]
            pairs = [
                (part(a, 0, hidden), part(wg, q * hidden, hidden)),
                (part(a, hidden, cut), part(wu, q * hidden, cut)),
                (part(b, 0, cut), part(wu, q * hidden + cut, cut)),
                (part(b, cut, hidden), part(wd, q * hidden, hidden)),
            ]
            if not (forward_blocks or has_back):
                pairs = pairs[:3]
            return [pltpu.make_async_copy(p, t, sems.at[i, q]) for i, (p, t) in enumerate(pairs)]

        for q in range(quarters):
            for copy in copies(q, places[2 * q], places[2 * q + 1]):
                copy.start()

        def load(index, carry):
            cols = columns(index)
            for b, terms in enumerate(picks):
                rows = block_rows(ins[terms[0][0]], terms[0][1], cols)
                for array, block in terms[1:]:
                    rows = rows + block_rows(ins[array], block, cols)
                x[b * size : (b + 1) * size, cols] = rows
            return carry

        lax.fori_loop(0, steps_of(width), load, 0)

        def add(rows, made, first):
            if not first:
                made = acc[rows] + made
            elif so_far is not None:
                made = base_ref[rows] + made
            acc[rows] = made

        def advance(q):
            for i in range(q * group, (q + 1) * group):
                for copy in copies(i, places[2 * i], places[2 * i + 1]):
                    copy.wait()
            first = q == 0
            part = slice(q * span, (q + 1) * span)
            if pre_blocks:
                rows = x[: pre_blocks * size]
                gate_pre = dot_nt(rows, wg[part])
                up_pre = dot_nt(rows, wu[part])
                for i, b in enumerate(keep):
                    keep_g[q, i * size : (i + 1) * size] = gate_pre[b * size : (b + 1) * size]
                    keep_u[q, i * size : (i + 1) * size] = up_pre[b * size : (b + 1) * size]
            if has_back:
                grad_act = dot_nt(x[grad * size : (grad + 1) * size], wd[part])
            if forward_blocks:
                count = forward_blocks * size
                fg = gate_pre[:count]
                act = (fg * jax.nn.sigmoid(fg) * up_pre[:count]).astype(BF16)
                made = dot(act, wd[part])
                add(slice(0, count), made, first)
            if has_back:
                base = forward_blocks * size
                if kept_pre is not None:
                    bg, bu = pre_g[q], pre_u[q]
                else:
                    bg = gate_pre[inner * size : (inner + 1) * size]
                    bu = up_pre[inner * size : (inner + 1) * size]
                sig = jax.nn.sigmoid(bg)
                grad_gate = (grad_act * bu * sig * (1.0 + bg * (1.0 - sig))).astype(BF16)
                grad_up = (grad_act * bg * sig).astype(BF16)
                made = dot(grad_gate, wg[part]) + dot(grad_up, wu[part])
                add(slice(base, base + size), made, first)

        for q in range(steps):
            advance(q)

        if outs and not partial:

            def store(index, carry):
                cols = columns(index)
                put_rows(out_ref, [acc[b * size : (b + 1) * size, cols] for b in range(outs)], cols)
                return carry

            lax.fori_loop(0, steps_of(width), store, 0)

    held_shape = pltpu.VMEM((quarters * hidden, width), BF16)
    passes = 2 * pre_blocks + forward_blocks + 3 * has_back
    return call(
        body,
        operands,
        shapes,
        [
            pltpu.VMEM((blocks * size, width), BF16),
            held_shape,
            held_shape,
            held_shape,
            pltpu.VMEM((max(outs, 1) * size, width), F32),
            pltpu.SemaphoreType.DMA((4, quarters)),
        ],
        2 * size * width * hidden * quarters * passes,
    )


def t_kept(dp_count, keeps, gain_pair, pick_pair):
    width = keeps[0][0].shape[-1]
    shape = jax.ShapeDtypeStruct((dp_count, 8, len(keeps) * CAP, width), BF16)

    def body(*refs):
        n = len(keeps)
        xs, pick_refs, (ga, gb), out = refs[:n], refs[n : 2 * n], refs[2 * n : 2 * n + 2], refs[-1]
        invs = [start_norm(x) for x in xs]

        def step(index, carry):
            cols = columns(index)
            blocks = []
            for x, inv, p in zip(xs, invs, pick_refs):
                v = by_half(x[:, cols].astype(F32) * inv, ga[:, cols], gb[:, cols]).astype(BF16)
                blocks.append(dot(p[...], v))
            for q in range(dp_count):
                put_rows(out.at[q], blocks, cols)
            return carry

        lax.fori_loop(0, steps_of(width), step, 0)

    return call(body, keeps + pick_pair + gain_pair, [shape], [], 10**8)[0]


def t_early(xs, pick_list, grads, gain_pair):
    width = xs[0][0].shape[-1]
    n, m = len(xs), len(grads)
    shape = jax.ShapeDtypeStruct((8, (n + m) * CAP, width), BF16)

    def body(*refs):
        x_refs, pick_refs = refs[:n], refs[n : 2 * n]
        grad_refs = refs[2 * n : 2 * n + 3 * m]
        ga, gb, out = refs[2 * n + 3 * m :]
        invs = [start_norm(x) for x in x_refs]

        def step(index, carry):
            cols = columns(index)
            blocks = []
            for x, inv, p in zip(x_refs, invs, pick_refs):
                v = by_half(x[:, cols].astype(F32) * inv, ga[:, cols], gb[:, cols]).astype(BF16)
                blocks.append(dot(p[...], v))
            for i in range(m):
                delta, p, gate = grad_refs[3 * i : 3 * i + 3]
                g = (gate[...] * delta[:, cols].astype(F32)).astype(BF16)
                blocks.append(dot(p[...], g))
            put_rows(out, blocks, cols)
            return carry

        lax.fori_loop(0, steps_of(width), step, 0)

    operands = xs + pick_list + [o for g in grads for o in g] + gain_pair
    return call(body, operands, [shape], [], 10**8)[0]


def t_inner(ret, keeps, spread_list, gate_list, pick_list, gain_pair):
    pair, width = keeps[0][0].shape[-2:]
    n = len(keeps)
    full = jax.ShapeDtypeStruct((pair, width), F32)
    shape = jax.ShapeDtypeStruct((8, n * CAP, width), BF16)

    def body(*refs):
        refs = list(refs)
        take = lambda k: [refs.pop(0) for _ in range(k)]
        back = take(1)[0]
        x_refs, spread_refs, gate_refs, pick_refs = take(n), take(n), take(n), take(n)
        ga, gb = take(2)
        mids = take(n)
        out = take(1)[0]
        invs = []
        for i in range(n):
            copies = back.shape[0] // 8
            spread = jnp.concatenate([spread_refs[i][...]] * copies, axis=1)
            gate = gate_refs[i][...]

            def step(index, total, i=i, spread=spread, gate=gate):
                cols = columns(index)
                m = x_refs[i][:, cols].astype(F32) + gate * dot(spread, block_rows(back, i, cols))
                mids[i][:, cols] = m
                return total + fold(m * m)

            total = lax.fori_loop(0, steps_of(width), step, jnp.zeros((pair, 128), F32))
            invs.append(inverse_rms(total, width))

        def step2(index, carry):
            cols = columns(index)
            blocks = []
            for i in range(n):
                v = by_half(mids[i][:, cols] * invs[i], ga[:, cols], gb[:, cols]).astype(BF16)
                blocks.append(dot(pick_refs[i][...], v))
            put_rows(out, blocks, cols)
            return carry

        lax.fori_loop(0, steps_of(width), step2, 0)

    operands = [ret] + keeps + spread_list + gate_list + pick_list + gain_pair
    return call(body, operands, [full] * n + [shape], [], 10**8)


def merge(place_ref, up, down, enter_refs, start, delta):
    tokens = up.shape[0] // 2
    bottom = place_ref[0] == 1
    top = place_ref[1] == 1

    def step(index, carry):
        cols = columns(index)
        ef = enter_refs[0]
        eg = enter_refs[1]
        low = slice(0, tokens)
        high = slice(tokens, 2 * tokens)
        load = lambda r, part: r[part, cols].astype(F32)
        start[low, cols] = jnp.where(bottom, load(ef, low), load(up, low))
        start[high, cols] = jnp.where(top, load(ef, high), load(down, low))
        delta[low, cols] = jnp.where(top, load(eg, low), load(down, high))
        delta[high, cols] = jnp.where(bottom, load(eg, high), load(up, high))
        return carry

    lax.fori_loop(0, steps_of(up.shape[1]), step, 0)


def t_middle(ret, start, delta, forward, backward, gain_pair, place=None, shifts=None, enters=None):
    width = ret[0].shape[-1]
    pair = backward[0][0].shape[-2]
    full = jax.ShapeDtypeStruct((pair, width), F32)
    shape = jax.ShapeDtypeStruct((8, 2 * CAP, width), BF16)
    shifted = place is not None

    def body(*refs):
        refs = list(refs)
        take = lambda k: [refs.pop(0) for _ in range(k)]
        if shifted:
            place_ref, up, down, ef, eg = take(5)
        else:
            start_ref, delta_ref = take(2)
        back = take(1)[0]
        spread_s, gate_s, pick_s, mid, spread_d, pick_d, gate_d, ga, gb = take(9)
        middle, inner, out, work = take(4)
        if shifted:
            merge(place_ref, up, down, (ef, eg), middle, inner)
            start_ref, delta_ref = middle, inner
        inv_s = add_routes(start_ref, back, 0, spread_s, gate_s, middle)
        factor, inv = back_sums(lambda c: mid[:, c], back, 1, spread_d, (ga, gb), work)

        def step(index, carry):
            cols = columns(index)
            v = by_half(middle[:, cols] * inv_s, ga[:, cols], gb[:, cols]).astype(BF16)
            d = delta_ref[:, cols].astype(F32) + inv * work[:, cols] - mid[:, cols] * factor
            inner[:, cols] = d
            g = (gate_d[...] * d).astype(BF16)
            put_rows(out, [dot(pick_s[...], v), dot(pick_d[...], g)], cols)
            return carry

        lax.fori_loop(0, steps_of(width), step, 0)

    first = [place] + shifts + enters if shifted else [start, delta]
    operands = first + [ret] + forward + backward + gain_pair
    return call(body, operands, [full, full, shape], [pltpu.VMEM((pair, width), F32)], 10**8)


def t_next(ret, middle, inner, kept, forward, backward, gain_pair, next_gains):
    width = ret[0].shape[-1]
    pair = kept[0].shape[-2]
    tokens = pair // 2
    ship = jax.ShapeDtypeStruct((pair, width), BF16)
    rows = jax.ShapeDtypeStruct((4, 2 * CAP, width), BF16)

    def body(*refs):
        refs = list(refs)
        take = lambda k: [refs.pop(0) for _ in range(k)]
        back, mid, inn, x = take(4)
        spread_s, gate_s, pick_s, spread_d, pick_d, gate_d, ga, gb, na, nb = take(10)
        up, down, rows_up, rows_down, work, ends = take(6)

        def finish(index, total):
            cols = columns(index)
            v = mid[:, cols] + gate_s[...] * dot(spread_s[...], block_rows(back, 0, cols))
            v = v.astype(BF16)
            up[:tokens, cols] = v[:tokens]
            down[:tokens, cols] = v[tokens:]
            v = v.astype(F32)
            ends[:, cols] = v
            return total + fold(v * v)

        total = lax.fori_loop(0, steps_of(width), finish, jnp.zeros((pair, 128), F32))
        inv_s = inverse_rms(total, width)
        factor, inv = back_sums(
            lambda c: x[:, c].astype(F32), back, 1, spread_d, (ga, gb), work
        )

        def step(index, carry):
            cols = columns(index)
            v = by_half(ends[:, cols] * inv_s, na[:, cols], nb[:, cols]).astype(BF16)
            d = inn[:, cols] + inv * work[:, cols] - x[:, cols].astype(F32) * factor
            d = d.astype(BF16)
            down[tokens:, cols] = d[:tokens]
            up[tokens:, cols] = d[tokens:]
            g = (gate_d[...] * d.astype(F32)).astype(BF16)
            blocks = [dot(pick_s[...], v), dot(pick_d[...], g)]
            put_rows(rows_up, blocks, cols)
            put_rows(rows_down, blocks, cols, rows_up.shape[0])
            return carry

        lax.fori_loop(0, steps_of(width), step, 0)

    big = pltpu.VMEM((pair, width), F32)
    operands = [ret, middle, inner, kept] + forward + backward + gain_pair + next_gains
    return call(body, operands, [ship, ship, rows, rows], [big, big], 10**8)


def t_last(ret, middle, inner, kept, forward, backward, gain_pair):
    width = ret[0].shape[-1]
    pair = kept[0].shape[-2]
    shape = jax.ShapeDtypeStruct((2 * pair, width), BF16)

    def body(*refs):
        refs = list(refs)
        take = lambda k: [refs.pop(0) for _ in range(k)]
        back, mid, inn, x, spread_s, gate_s, spread_d, ga, gb, out, work = refs
        factor, inv = back_sums(
            lambda c: x[:, c].astype(F32), back, 1, spread_d, (ga, gb), work
        )

        def step(index, carry):
            cols = columns(index)
            f = mid[:, cols] + gate_s[...] * dot(spread_s[...], block_rows(back, 0, cols))
            out[:pair, cols] = f.astype(BF16)
            v = inn[:, cols] + inv * work[:, cols] - x[:, cols].astype(F32) * factor
            out[pair:, cols] = v.astype(BF16)
            return carry

        lax.fori_loop(0, steps_of(width), step, 0)

    operands = [ret, middle, inner, kept] + forward + backward + gain_pair
    return call(body, operands, [shape], [pltpu.VMEM((pair, width), F32)], 10**8)[0]


def local(state_in, entering, saved, route_ids, gate_vals, w_gate, w_up, w_down, gains):
    width = state_in.shape[-1]
    tokens = state_in.shape[-2]
    pair = 2 * tokens
    hidden = w_down.shape[-2]
    dp_count = lax.axis_size("dp")
    segment_count = lax.axis_size("segment")
    expert_devices = lax.axis_size("expert")
    section = lax.axis_index("segment").astype(jnp.int32)
    at_bottom = (section == 0).astype(jnp.int32)
    at_top = (section == segment_count - 1).astype(jnp.int32)
    place = jnp.stack([at_bottom, at_top])

    cut = hidden // 2
    turned_up = jnp.transpose(w_up[0, 0])
    own_a = jnp.concatenate([jnp.transpose(w_gate[0, 0]), turned_up[:cut]])
    own_b = jnp.concatenate([turned_up[cut:], w_down[0, 0]])
    ahead = [(i, (i + 1) % dp_count) for i in range(dp_count)]
    behind = [((i + 1) % dp_count, i) for i in range(dp_count)]
    left_a = lax.ppermute(own_a, "dp", ahead)
    right_b = lax.ppermute(own_b, "dp", behind)
    left_b = lax.ppermute(own_b, "dp", ahead)
    right_a = lax.ppermute(own_a, "dp", behind)

    def exchange(blocks):
        return lax.all_to_all(blocks, "expert", split_axis=0, concat_axis=0, tiled=True)

    upward = [(i, i + 1) for i in range(segment_count - 1)]
    downward = [(i + 1, i) for i in range(segment_count - 1)]

    def paired(values):
        turned = jnp.transpose(values[0], (0, 1, 4, 2, 3))
        stream_a = turned[:, 0::2]
        stream_b = jnp.flip(turned[:, 1::2], axis=3)
        both = jnp.concatenate([stream_a, stream_b], axis=4)
        both = jnp.transpose(both, (0, 1, 3, 2, 4))
        return both.reshape((8,) + both.shape[3:])

    own_a, own_b, route_ids, gate_vals = lax.optimization_barrier((own_a, own_b, route_ids, gate_vals))
    ids = paired(route_ids).astype(F32)
    gates = paired(gate_vals)
    choices = ids.shape[1]
    gain_rows = gains[0].reshape(2, width // 128, 128)
    pack_down = jnp.concatenate(
        [ids[4, :, :tokens], ids[7, :, tokens:], gates[4, :, :tokens], gates[7, :, tokens:], gain_rows[0]]
    )
    pack_up = jnp.concatenate(
        [ids[7, :, :tokens], ids[4, :, tokens:], gates[7, :, :tokens], gates[4, :, tokens:], gain_rows[1]]
    )
    above = lax.ppermute(pack_down, "segment", downward)
    below = lax.ppermute(pack_up, "segment", upward)
    part = lambda v, i: v[i * choices : (i + 1) * choices]
    more_ids = jnp.stack(
        [
            jnp.concatenate([part(above, 0), part(below, 1)], axis=1),
            jnp.concatenate([part(below, 0), part(above, 1)], axis=1),
        ]
    )
    more_gates = jnp.stack(
        [
            jnp.concatenate([part(above, 2), part(below, 3)], axis=1),
            jnp.concatenate([part(below, 2), part(above, 3)], axis=1),
        ]
    )
    gain_above = above[4 * choices :].reshape(1, width)
    gain_below = below[4 * choices :].reshape(1, width)
    all_ids = jnp.concatenate([ids, more_ids]).astype(jnp.int32)
    all_gates = jnp.concatenate([gates, more_gates])
    picks, spreads, gate_columns = make_tables(place, all_ids, all_gates)

    pick = lambda t: (picks, item(picks.shape, (t,)))
    spread = lambda t: (spreads, item(spreads.shape, (t,)))
    gate = lambda t: (gate_columns, item(gate_columns.shape, (t,)))
    gain_lines = gains[0].reshape(2, 1, width)
    gain = lambda j: (gain_lines, item(gain_lines.shape, (j,)))
    plain = lambda a: (a, whole(a.shape))
    states = state_in.reshape(2, pair, width)
    state = lambda p: (states, item(states.shape, (p,)))
    keeps = saved.reshape(2, pair, width)
    kept = lambda t: (keeps, item(keeps.shape, (t,)))
    enters = entering.reshape(2, pair, width)
    enter = lambda p: (enters, item(enters.shape, (p,)))
    place_in = (place, pl.BlockSpec(memory_space=pltpu.SMEM))
    first_gains = [gain(0), gain(1)]
    second_gains = [gain(1), gain(0)]

    def exchange_all(rows):
        return lax.all_to_all(rows, ("dp", "expert"), split_axis=0, concat_axis=0, tiled=True)

    rows0 = t_kept(dp_count, [kept(0), kept(1)], first_gains, [pick(2), pick(6)])
    got0 = exchange_all(rows0.reshape((dp_count * expert_devices,) + rows0.shape[2:]))
    got0, left_a, right_b = lax.optimization_barrier((got0, left_a, right_b))
    far_a = lax.ppermute(left_a, "dp", ahead)
    far_b = lax.ppermute(right_b, "dp", behind)
    rows_e = t_early(
        [state(0), kept(0), kept(1)],
        [pick(0), pick(2), pick(6)],
        [(state(1), pick(3), gate(3))],
        first_gains,
    )
    got_e = exchange(rows_e)
    (out0,) = owner_call(
        [own_a, own_b], [got0], [[(0, 0)], [(0, 1)]], 2, 2, None, None, None, (), 2
    )
    out0, got_e = lax.optimization_barrier((out0, got_e))
    ret0 = exchange_all(out0)

    late_enters, left_b, right_a = lax.optimization_barrier((enters, left_b, right_a))
    weights = [own_a, own_b, left_a, left_b, right_a, right_b, far_a, far_b]
    late = lambda p: (late_enters, item(enters.shape, (p,)))
    rows_end = t_early([late(0)], [pick(10)], [(late(1), pick(11), gate(7))], first_gains)
    mid_kept0, mid_kept1, rows_i = t_inner(
        plain(ret0),
        [kept(0), kept(1)],
        [spread(2), spread(6)],
        [gate(2), gate(6)],
        [pick(3), pick(7)],
        second_gains,
    )
    rows_i, rows_end = lax.optimization_barrier((rows_i, rows_end))
    got_i = exchange(rows_i)

    rows1 = [[(0, 0)], [(1, 0)], [(0, 3)]]
    (near,) = owner_call(
        weights[:-2], [got_e, got_i], rows1, 2, 1, 2, 1, None, (), 2, partial=True
    )
    (out1,) = owner_call(weights[-2:], [got_e, got_i], rows1, 2, 1, 2, 1, None, (), 2, near)
    pre_g, pre_u = owner_call(
        weights, [got_e, got_i], [[(0, 1)], [(0, 2)], [(1, 1)]], 3, 0, None, None, None, (0, 1, 2), 0
    )
    ret1 = exchange(out1)
    middle0, inner0, rows2 = t_middle(
        plain(ret1),
        state(0),
        state(1),
        [spread(0), gate(0), pick(1)],
        [plain(mid_kept0), spread(3), pick(2), gate(2)],
        second_gains,
    )

    got2 = exchange(rows2)
    both = [[(0, 0)], [(0, 1)]]
    (out2,) = owner_call(weights, [got2], both, 1, 1, 1, None, (pre_g, pre_u, 0), (), 2)
    ret2 = exchange(out2)
    ship_up, ship_down, rows_up, rows_down = t_next(
        plain(ret2),
        plain(middle0),
        plain(inner0),
        kept(0),
        [spread(1), gate(1), pick(8)],
        [spread(2), pick(9), gate(9)],
        first_gains,
        [plain(gain_above), plain(gain_below)],
    )

    from_below = lax.ppermute(rows_up, "segment", upward)
    from_above = lax.ppermute(rows_down, "segment", downward)
    rows3 = jnp.concatenate([from_below, from_above]) + rows_end
    ship_up, ship_down, rows3 = lax.optimization_barrier((ship_up, ship_down, rows3))
    shift_up = lax.ppermute(ship_up, "segment", upward)
    shift_down = lax.ppermute(ship_down, "segment", downward)
    got3 = exchange(rows3)
    (out3,) = owner_call(weights, [got3], both, 1, 1, 1, None, (pre_g, pre_u, 2), (), 2)
    ret3 = exchange(out3)
    middle1, inner1, rows4 = t_middle(
        plain(ret3),
        None,
        None,
        [spread(4), gate(4), pick(5)],
        [plain(mid_kept1), spread(7), pick(6), gate(6)],
        second_gains,
        place_in,
        [plain(shift_up), plain(shift_down)],
        [enter(0), enter(1)],
    )

    got4 = exchange(rows4)
    (out4,) = owner_call(weights, [got4], both, 1, 1, 1, None, (pre_g, pre_u, 1), (), 2)
    ret4 = exchange(out4)
    result = t_last(
        plain(ret4),
        plain(middle1),
        plain(inner1),
        kept(1),
        [spread(5), gate(5)],
        [spread(6)],
        first_gains,
    )
    return result.reshape(state_in.shape)


def solution(mesh):
    in_specs = (
        P("segment", None, ("expert", "dp"), None),
        P(None, None, ("expert", "dp"), None),
        P("segment", None, None, ("expert", "dp"), None),
        P("segment", None, None, None, ("expert", "dp"), None),
        P("segment", None, None, None, ("expert", "dp"), None),
        P("segment", "expert", None, "dp"),
        P("segment", "expert", None, "dp"),
        P("segment", "expert", "dp", None),
        P("segment", None, None),
    )
    out_specs = P("segment", None, ("expert", "dp"), None)
    return jax.shard_map(local, mesh=mesh, in_specs=in_specs, out_specs=out_specs, check_vma=False)
```
